32 devices in a mesh: mode: 4 (over y, core), blk: 8 (over z, x).
Axes of the slice: x: 2, y: 2, z: 4, core: 2. Of those that a mesh axis runs over, the one named last changes fastest.
Arguments:
- divergence: float32 [8, 32, 128, 1024], P('blk', None, 'mode')
- neighbours: int32 [8, 2], P('blk'), may hold values from -1 to 7, as said below
- levels: int32 [8], P('blk'), may hold values from 0 to 2
- sweeps: int32 [3], replicated, may hold values from 1 to 2, as said below
Outputs:
- pressure: float32 [8, 32, 128, 1024], P('blk', None, 'mode')
The draws below stay inside these ranges and needn't reach their ends.
Inputs may be any that keep to these rules, and one draw needn't show every extreme that they name: `neighbours`: row b holds the slots of the columns west (entry 0) and east (entry 1) of the column in slot b along x, -1 beyond the two ends of the 8 columns. The lists are mutual, every slot is named, and every neighbour's slot lies within 3 of b, exactly 3 away for some. Some level has 2 sweeps.
All inputs are finite; a program needn't handle non-finite values.
Results may differ from the reference program's by a relative error of at most 0.0003.
Values sent between devices are 32-bit elements; how exact they have to be, the bound alone decides.
A program may use at most 128 MiB of HBM per device.

```python
import math
import jax
import jax.numpy as jnp
from jax import lax

NY = 1024
BX = 32
NZ = 128
SWEEPS = 2
LEVELS = 3
CITERS = 8
COLS = 8
N_MODE = 4


def draw_divergence(key, part):
    shape = (COLS, BX, NZ, NY)
    return jax.random.normal(key, shape, jnp.float32)


def draw_neighbours(key, part):
    pair_count = COLS // 2
    swapped = jax.random.randint(key, (pair_count,), 0, 2).astype(jnp.int32)
    forced = jax.random.randint(jax.random.fold_in(key, 3), (), 0, pair_count - 1).astype(jnp.int32)
    group_ids = jnp.arange(pair_count, dtype=jnp.int32)
    swapped = jnp.where((group_ids == forced) | (group_ids == forced + 1), 1, swapped).astype(jnp.int32)
    positions = jnp.arange(COLS, dtype=jnp.int32)
    slot_of = 2 * (positions // 2) + (positions % 2 ^ swapped[positions // 2])
    west_pos = positions - 1
    east_pos = positions + 1
    west_slot = jnp.where(west_pos >= 0, slot_of[jnp.clip(west_pos, 0, COLS - 1)], -1)
    east_slot = jnp.where(east_pos < COLS, slot_of[jnp.clip(east_pos, 0, COLS - 1)], -1)
    table = jnp.zeros((COLS, 2), jnp.int32)
    table = table.at[slot_of, 0].set(west_slot.astype(jnp.int32))
    table = table.at[slot_of, 1].set(east_slot.astype(jnp.int32))
    return table


def draw_sweeps(key, part):
    counts = jax.random.randint(key, (LEVELS,), 1, SWEEPS + 1).astype(jnp.int32)
    chosen = jax.random.randint(jax.random.fold_in(key, 5), (), 0, LEVELS).astype(jnp.int32)
    return jnp.where(jnp.arange(LEVELS, dtype=jnp.int32) == chosen, SWEEPS, counts).astype(jnp.int32)


def with_ends(array, stream_key, least, top_value):
    longest = array.shape.index(max(array.shape))
    spots = []
    for shift in (0, 1):
        where = [jax.random.randint(jax.random.fold_in(stream_key, axis), (), 0, length) for axis, length in enumerate(array.shape)]
        where[longest] = (where[longest] + shift) % array.shape[longest]
        spots.append(tuple(where))
    return array.at[spots[0]].set(least).at[spots[1]].set(top_value)


def setup_inputs(seed: int = 0) -> dict:
    arg_keys = jax.random.split(jax.random.key(seed), 5)
    divergence = draw_divergence(jax.random.fold_in(arg_keys[4], 71), 0)
    neighbours = draw_neighbours(jax.random.fold_in(arg_keys[4], 71), 0)
    levels = with_ends(jax.random.randint(arg_keys[2], (COLS,), 0, LEVELS), jax.random.fold_in(arg_keys[2], 1), 0, LEVELS - 1).astype(jnp.int32)
    sweeps = draw_sweeps(jax.random.fold_in(arg_keys[4], 71), 0)
    return {"divergence": divergence, "neighbours": neighbours, "levels": levels, "sweeps": sweeps}


PRECISE = lax.Precision.HIGHEST
DAMPING = 0.8

def sine_table(extent):
    ordinal = jnp.arange(extent, dtype=jnp.int32) + 1
    phases = ordinal[:, None] * ordinal[None, :] % (2 * (extent + 1))
    angles = phases.astype(jnp.float32) * (math.pi / (extent + 1))
    matrix = math.sqrt(2.0 / (extent + 1)) * jnp.sin(angles)
    spectrum = 2.0 - 2.0 * jnp.cos(ordinal.astype(jnp.float32) * (math.pi / (extent + 1)))
    return (matrix.astype(jnp.float32), spectrum.astype(jnp.float32))

def fourier_table(length):
    half_len = length // 2
    row_ids = jnp.arange(length, dtype=jnp.int32)
    wavenumber = jnp.where(row_ids <= half_len, row_ids, row_ids - half_len)
    phases = wavenumber[:, None] * row_ids[None, :] % length
    angles = phases.astype(jnp.float32) * (2.0 * math.pi / length)
    fourier = jnp.where((row_ids <= half_len)[:, None], jnp.cos(angles), jnp.sin(angles)).astype(jnp.float32)
    edges = (row_ids == 0) | (row_ids == half_len)
    weights = jnp.where(edges, 1.0 / length, 2.0 / length).astype(jnp.float32)
    wave_shift = (2.0 - 2.0 * jnp.cos(wavenumber.astype(jnp.float32) * (2.0 * math.pi / length))).astype(jnp.float32)
    return (fourier, weights, wave_shift)

def stiffness_of(levels):
    return jnp.left_shift(jnp.ones_like(levels), 2 * levels).astype(jnp.float32)

def local_solve(loaded, stiffness, wave_shift, tables):
    sine_x, lambda_x, sine_z, lambda_z = tables
    transformed = jnp.einsum('bxzq,xi->bizq', loaded, sine_x, precision=PRECISE)
    transformed = jnp.einsum('bizq,zj->bijq', transformed, sine_z, precision=PRECISE)
    divisor = stiffness[:, None, None, None] * (lambda_x[None, :, None, None] + lambda_z[None, None, :, None]) + wave_shift[None, None, None, :]
    transformed = transformed / divisor
    transformed = jnp.einsum('bijq,ix->bxjq', transformed, sine_x, precision=PRECISE)
    return jnp.einsum('bxjq,jz->bxzq', transformed, sine_z, precision=PRECISE)

def apply_local(iterate, stiffness, wave_shift):
    padded_x = jnp.pad(iterate, ((0, 0), (1, 1), (0, 0), (0, 0)))
    padded_z = jnp.pad(iterate, ((0, 0), (0, 0), (1, 1), (0, 0)))
    laplace = 4.0 * iterate - padded_x[:, 2:] - padded_x[:, :-2] - padded_z[:, :, 2:] - padded_z[:, :, :-2]
    return stiffness[:, None, None, None] * laplace + wave_shift * iterate

def boundary(iterate, neighbours):
    west_slot = neighbours[:, 0]
    east_slot = neighbours[:, 1]
    west_present = (west_slot >= 0).astype(jnp.float32)[:, None, None]
    east_present = (east_slot >= 0).astype(jnp.float32)[:, None, None]
    from_west = jnp.take(iterate[:, -1], jnp.maximum(west_slot, 0), axis=0) * west_present
    from_east = jnp.take(iterate[:, 0], jnp.maximum(east_slot, 0), axis=0) * east_present
    return (from_west, from_east)

def loaded_rhs(source, from_west, from_east, stiffness):
    factor = stiffness[:, None, None]
    loaded = source.at[:, 0].add(factor * from_west)
    return loaded.at[:, -1].add(factor * from_east)

def neighbour_sum(values, neighbours):
    west_slot = neighbours[:, 0]
    east_slot = neighbours[:, 1]
    west_present = (west_slot >= 0).astype(jnp.float32)[:, None]
    east_present = (east_slot >= 0).astype(jnp.float32)[:, None]
    return jnp.take(values, jnp.maximum(west_slot, 0), axis=0) * west_present + jnp.take(values, jnp.maximum(east_slot, 0), axis=0) * east_present

def coarse_terms(stiffness, wave_shift):
    diagonal = stiffness[:, None] * float(2 * NZ + 2 * BX) + float(BX * NZ) * wave_shift[None, :]
    coupling = stiffness[:, None] * float(NZ)
    return (diagonal, coupling)

def reference(divergence, neighbours, levels, sweeps):
    fourier, weights, wave_shift = fourier_table(NY)
    tables = sine_table(BX) + sine_table(NZ)
    stiffness = stiffness_of(levels)
    allowed = jnp.take(sweeps, levels)
    spectrum = jnp.einsum('bxzy,qy->bxzq', divergence, fourier, precision=PRECISE)
    share = NY // N_MODE
    blocks = NY // share
    spectrum = jnp.moveaxis(spectrum.reshape(COLS, BX, NZ, blocks, share), 3, 0)
    shifts = wave_shift.reshape(blocks, share)

    def smooth(iterate, source, own_shift):
        for repeat in range(SWEEPS):
            from_west, from_east = boundary(iterate, neighbours)
            solved = local_solve(loaded_rhs(source, from_west, from_east, stiffness), stiffness, own_shift, tables)
            iterate = jnp.where((allowed > repeat)[:, None, None, None], solved, iterate)
        return iterate

    def cycle(block_pair):
        source, own_shift = block_pair
        iterate = smooth(jnp.zeros_like(source), source, own_shift)
        from_west, from_east = boundary(iterate, neighbours)
        remainder = loaded_rhs(source, from_west, from_east, stiffness) - apply_local(iterate, stiffness, own_shift)
        coarse_rhs = lax.optimization_barrier(jnp.sum(remainder, axis=(1, 2)))
        diagonal, coupling = coarse_terms(stiffness, own_shift)
        correction = jnp.zeros_like(coarse_rhs)
        for repeat in range(CITERS):
            beside = neighbour_sum(correction, neighbours)
            correction = correction + DAMPING * (coarse_rhs - diagonal * correction + coupling * beside) / diagonal
        iterate = iterate + correction[:, None, None, :]
        return smooth(iterate, source, own_shift)
    solved_blocks = lax.map(cycle, (spectrum, shifts))
    solution = jnp.moveaxis(solved_blocks, 0, 3).reshape(COLS, BX, NZ, NY)
    return jnp.einsum('bxzq,qy->bxzy', solution * weights, fourier, precision=PRECISE)
```

```python
import jax
import jax.numpy as jnp
import numpy as np
from jax import lax
from jax.sharding import PartitionSpec as P

SWEEPS = 2
CITERS = 8
DAMPING = 0.8
HIGH = lax.Precision.HIGH
HIGHEST = lax.Precision.HIGHEST


def sine_table(extent):
    ordinal = np.arange(1, extent + 1)
    phases = np.outer(ordinal, ordinal) % (2 * (extent + 1))
    matrix = np.sqrt(2.0 / (extent + 1)) * np.sin(phases * (np.pi / (extent + 1)))
    eigen = 2.0 - 2.0 * np.cos(ordinal * (np.pi / (extent + 1)))
    return matrix, eigen


def fourier_table(length):
    half = length // 2
    ids = np.arange(length)
    wave = np.where(ids <= half, ids, ids - half)
    angles = (np.outer(wave, ids) % length) * (2.0 * np.pi / length)
    fourier = np.where((ids <= half)[:, None], np.cos(angles), np.sin(angles))
    weights = np.where((ids == 0) | (ids == half), 1.0, 2.0) / length
    shift = 2.0 - 2.0 * np.cos(wave * (2.0 * np.pi / length))
    return fourier, weights, shift


def f32(array):
    return jnp.asarray(np.asarray(array, np.float32))


def face_response(mu, extent):
    half = 0.5 * mu
    rho = 1.0 / (1.0 + half + jnp.sqrt(mu + half * half))
    rho2 = rho * rho
    power = jnp.ones_like(rho)
    base, left = rho, extent
    while left:
        if left & 1:
            power = power * base
        base, left = base * base, left >> 1
    scale = 1.0 / (1.0 - power * power * rho2)
    return rho * (1.0 - power * power) * scale, power * (1.0 - rho2) * scale


def vcycle(first_face, last_face, table, mu, sums, stiffness, allowed, shift):
    columns = first_face.shape[0]
    ids = jnp.arange(columns, dtype=jnp.int32)
    west_hot = (table[:, :1] == ids[None, :]).astype(jnp.float32)
    east_hot = (table[:, 1:2] == ids[None, :]).astype(jnp.float32)

    def beside(hot, values):
        return jnp.sum(hot.reshape(hot.shape + (1,) * (values.ndim - 1)) * values[None], axis=1)

    direct, across = face_response(mu, direct_extent(sums))
    twice = (allowed > 1)[:, None, None]

    def sweep(west, east):
        return (
            first_face + direct * west + across * east,
            last_face + across * west + direct * east,
        )

    used_w, used_e = beside(west_hot, last_face), beside(east_hot, first_face)
    second = sweep(used_w, used_e)
    first = jnp.where(twice, second[0], first_face)
    last = jnp.where(twice, second[1], last_face)
    west, east = beside(west_hot, last), beside(east_hot, first)
    zero = jnp.zeros_like(west)
    change = west + east - jnp.where(twice, used_w + used_e, zero)
    part = jnp.sum(change * sums["z"][None, :, None], axis=1)
    rhs = lax.psum(part, "blk") * stiffness[:, None]
    diagonal = stiffness[:, None] * sums["perimeter"] + sums["cells"] * shift[None, :]
    coupling = stiffness[:, None] * sums["extent_z"]
    link = west_hot + east_hot
    correction = DAMPING * rhs / diagonal
    for _ in range(CITERS - 1):
        correction = (
            correction
            + DAMPING * (rhs - diagonal * correction + coupling * beside(link, correction)) / diagonal
        )
    west = west + beside(west_hot, correction)[:, None, :] * sums["z"][None, :, None]
    east = east + beside(east_hot, correction)[:, None, :] * sums["z"][None, :, None]
    first, last = sweep(west, east)
    again_w, again_e = beside(west_hot, last), beside(east_hot, first)
    return jnp.where(twice, again_w, west), jnp.where(twice, again_e, east)


def direct_extent(sums):
    return sums["extent_x"]


def body(divergence, neighbours, levels, sweeps):
    _, bx, nl, ny = divergence.shape
    modes = lax.axis_size("mode")
    columns = lax.axis_size("blk")
    nz = nl * modes
    nq = ny // modes
    jb = nz // columns
    fourier, weights, shift = fourier_table(ny)
    sx, lx = sine_table(bx)
    sz, lz = sine_table(nz)
    sl, ll = sine_table(nl)
    both = np.kron(sx, sl)
    to_global = sz @ np.kron(np.eye(modes), sl)
    rows = [r for d in range(1, modes) for r in (d * nl - 1, d * nl)]
    ends = f32(sz[rows])
    s0, s1 = f32(sx[0]), f32(sx[-1])
    e0, e1 = f32(sl[0]), f32(sl[-1])
    k = f32(shift)
    blk = lax.axis_index("blk")
    own_k = lax.dynamic_slice_in_dim(k, lax.axis_index("mode") * nq, nq)

    facts = lax.all_gather(
        jnp.concatenate([neighbours[0], levels])[None], "blk", axis=0, tiled=True
    )
    all_levels = facts[:, 2]
    level_ids = jnp.arange(sweeps.shape[0], dtype=jnp.int32)
    allowed = jnp.sum(jnp.where(all_levels[:, None] == level_ids, sweeps, 0), axis=1)
    all_s = jnp.left_shift(jnp.ones_like(all_levels), 2 * all_levels).astype(jnp.float32)
    s = jnp.left_shift(jnp.ones_like(levels), 2 * levels).astype(jnp.float32)[0]

    cells = divergence.reshape(bx * nl, ny)
    spectrum = jnp.dot(cells, f32(fourier.T), precision=HIGH)
    ghat = jnp.dot(f32(both), spectrum, precision=HIGH).reshape(bx, nl, ny)
    local = s * (f32(lx)[:, None, None] + f32(ll)[None, :, None]) + k
    vhat = ghat / local
    out = jnp.concatenate(
        [
            jnp.sum(vhat * e0[None, :, None], axis=1),
            jnp.sum(vhat * e1[None, :, None], axis=1),
            jnp.sum(vhat * s0[:, None, None], axis=0),
            jnp.sum(vhat * s1[:, None, None], axis=0),
        ]
    )
    out = jnp.stack([out[:, d * nq : (d + 1) * nq] for d in range(modes)])
    got = lax.all_to_all(out, "mode", split_axis=0, concat_axis=0)
    vf, vl = got[:, :bx], got[:, bx : 2 * bx]
    a0 = got[:, 2 * bx : 2 * bx + nl].reshape(nz, nq)
    a1 = got[:, 2 * bx + nl :].reshape(nz, nq)
    jump = jnp.stack([t for d in range(1, modes) for t in (vf[d], vl[d - 1])])
    jump = jnp.einsum("rj,riq->ijq", ends, jump, precision=HIGHEST)
    whole = s * (f32(lx)[:, None, None] + f32(lz)[None, :, None]) + own_k
    lift = s * jump / whole
    m = f32(to_global)
    face0 = jnp.dot(m, a0, precision=HIGHEST) + jnp.sum(lift * s0[:, None, None], axis=0)
    face1 = jnp.dot(m, a1, precision=HIGHEST) + jnp.sum(lift * s1[:, None, None], axis=0)
    faces = jnp.stack([face0.reshape(columns, jb, nq), face1.reshape(columns, jb, nq)], axis=1)
    faces = lax.all_to_all(faces, "blk", split_axis=0, concat_axis=0)

    own_lz = lax.dynamic_slice_in_dim(f32(lz), blk * jb, jb)
    sums = {
        "z": lax.dynamic_slice_in_dim(f32(sz.sum(axis=0)), blk * jb, jb),
        "perimeter": float(2 * nz + 2 * bx),
        "cells": float(bx * nz),
        "extent_z": float(nz),
        "extent_x": bx,
    }
    mu = own_lz[None, :, None] + own_k[None, None, :] / all_s[:, None, None]
    west, east = vcycle(faces[:, 0], faces[:, 1], facts[:, :2], mu, sums, all_s, allowed, own_k)
    back = lax.all_to_all(jnp.stack([west, east], axis=1), "blk", split_axis=0, concat_axis=0)
    west, east = back[:, 0].reshape(nz, nq), back[:, 1].reshape(nz, nq)

    total = lift + s * (s0[:, None, None] * west + s1[:, None, None] * east) / whole
    inner = jnp.einsum("rj,ijq->riq", ends, total, precision=HIGHEST)
    none = jnp.zeros((bx, nq), jnp.float32)
    mt = f32(to_global.T)
    west = jnp.dot(mt, west, precision=HIGHEST).reshape(modes, nl, nq)
    east = jnp.dot(mt, east, precision=HIGHEST).reshape(modes, nl, nq)
    parcels = []
    for d in range(modes):
        below = none if d == 0 else inner[2 * d - 2] + vl[d - 1]
        above = none if d == modes - 1 else inner[2 * d + 1] + vf[d + 1]
        parcels.append(jnp.concatenate([below, above, west[d], east[d]]))
    got = lax.all_to_all(jnp.stack(parcels), "mode", split_axis=0, concat_axis=0)
    got = jnp.concatenate([got[d] for d in range(modes)], axis=1)
    below, above = got[:bx], got[bx : 2 * bx]
    west, east = got[2 * bx : 2 * bx + nl], got[2 * bx + nl :]
    full = ghat + s * (
        s0[:, None, None] * west[None]
        + s1[:, None, None] * east[None]
        + e0[None, :, None] * below[:, None]
        + e1[None, :, None] * above[:, None]
    )
    full = (full / local).reshape(bx * nl, ny)
    cells = jnp.dot(f32(both), full, precision=HIGH)
    pressure = jnp.dot(cells, f32(weights[:, None] * fourier), precision=HIGH)
    return pressure.reshape(divergence.shape)


def solution(mesh):
    return jax.shard_map(
        body,
        mesh=mesh,
        in_specs=(P("blk", None, "mode", None), P("blk", None), P("blk"), P()),
        out_specs=P("blk", None, "mode", None),
        check_vma=False,
    )
```

```python
import functools

import jax
import jax.numpy as jnp
import numpy as np
from jax import lax
from jax.experimental import pallas as pl
from jax.experimental.pallas import tpu as pltpu
from jax.sharding import PartitionSpec as P

SWEEPS = 2
CITERS = 8
DAMPING = 0.8
HIGH = lax.Precision.HIGH
HIGHEST = lax.Precision.HIGHEST


def sine_table(extent):
    ordinal = np.arange(1, extent + 1)
    phases = np.outer(ordinal, ordinal) % (2 * (extent + 1))
    matrix = np.sqrt(2.0 / (extent + 1)) * np.sin(phases * (np.pi / (extent + 1)))
    eigen = 2.0 - 2.0 * np.cos(ordinal * (np.pi / (extent + 1)))
    return matrix, eigen


def fourier_table(length):
    half = length // 2
    ids = np.arange(length)
    wave = np.where(ids <= half, ids, ids - half)
    angles = (np.outer(wave, ids) % length) * (2.0 * np.pi / length)
    fourier = np.where((ids <= half)[:, None], np.cos(angles), np.sin(angles))
    weights = np.where((ids == 0) | (ids == half), 1.0, 2.0) / length
    shift = 2.0 - 2.0 * np.cos(wave * (2.0 * np.pi / length))
    return fourier, weights, shift


def f32(array):
    return jnp.asarray(np.asarray(array, np.float32))


def exchange_kernel(axis, n, same, src, dst, send_sem, recv_sem, own_sem):
    me = lax.axis_index(axis)
    barrier = pltpu.get_barrier_semaphore()
    for step in range(1, n):
        peer = lax.rem(me + step, n)
        pl.semaphore_signal(
            barrier, inc=1, device_id={axis: peer}, device_id_type=pl.DeviceIdType.MESH
        )
    own = pltpu.make_async_copy(src if same else src.at[me], dst.at[me], own_sem)
    own.start()
    pl.semaphore_wait(barrier, n - 1)
    copies = []
    for step in range(1, n):
        peer = lax.rem(me + step, n)
        copy = pltpu.make_async_remote_copy(
            src_ref=src if same else src.at[peer],
            dst_ref=dst.at[me],
            send_sem=send_sem.at[step],
            recv_sem=recv_sem.at[step],
            device_id={axis: peer},
            device_id_type=pl.DeviceIdType.MESH,
        )
        copy.start()
        copies.append(copy)
    own.wait()
    for copy in copies:
        copy.wait()


def exchange(values, axis, number, same=False):
    n = lax.axis_size(axis)
    block = values.shape if same else values.shape[1:]
    return pl.pallas_call(
        functools.partial(exchange_kernel, axis, n, same),
        out_shape=jax.ShapeDtypeStruct((n,) + block, values.dtype),
        in_specs=[pl.BlockSpec(memory_space=pltpu.VMEM)],
        out_specs=pl.BlockSpec(memory_space=pltpu.VMEM),
        scratch_shapes=[
            pltpu.SemaphoreType.DMA((n,)),
            pltpu.SemaphoreType.DMA((n,)),
            pltpu.SemaphoreType.DMA,
        ],
        compiler_params=pltpu.CompilerParams(collective_id=number, has_side_effects=True),
        name=f"exchange_{axis}_{number}",
    )(values)


def face_response(mu, extent):
    half = 0.5 * mu
    rho = 1.0 / (1.0 + half + jnp.sqrt(mu + half * half))
    rho2 = rho * rho
    power = jnp.ones_like(rho)
    base, left = rho, extent
    while left:
        if left & 1:
            power = power * base
        base, left = base * base, left >> 1
    scale = 1.0 / (1.0 - power * power * rho2)
    return rho * (1.0 - power * power) * scale, power * (1.0 - rho2) * scale


def vcycle(first_face, last_face, table, mu, sums, stiffness, allowed, shift):
    columns = first_face.shape[0]
    ids = jnp.arange(columns, dtype=jnp.int32)
    west_hot = (table[:, :1] == ids[None, :]).astype(jnp.float32)
    east_hot = (table[:, 1:2] == ids[None, :]).astype(jnp.float32)

    def beside(hot, values):
        return jnp.sum(hot.reshape(hot.shape + (1,) * (values.ndim - 1)) * values[None], axis=1)

    direct, across = face_response(mu, direct_extent(sums))
    twice = (allowed > 1)[:, None, None]

    def sweep(west, east):
        return (
            first_face + direct * west + across * east,
            last_face + across * west + direct * east,
        )

    used_w, used_e = beside(west_hot, last_face), beside(east_hot, first_face)
    second = sweep(used_w, used_e)
    first = jnp.where(twice, second[0], first_face)
    last = jnp.where(twice, second[1], last_face)
    west, east = beside(west_hot, last), beside(east_hot, first)
    zero = jnp.zeros_like(west)
    change = west + east - jnp.where(twice, used_w + used_e, zero)
    part = jnp.sum(change * sums["z"][None, :, None], axis=1)
    rhs = jnp.sum(exchange(part, "blk", 2, same=True), axis=0) * stiffness[:, None]
    diagonal = stiffness[:, None] * sums["perimeter"] + sums["cells"] * shift[None, :]
    coupling = stiffness[:, None] * sums["extent_z"]
    link = west_hot + east_hot
    correction = DAMPING * rhs / diagonal
    for _ in range(CITERS - 1):
        correction = (
            correction
            + DAMPING * (rhs - diagonal * correction + coupling * beside(link, correction)) / diagonal
        )
    west = west + beside(west_hot, correction)[:, None, :] * sums["z"][None, :, None]
    east = east + beside(east_hot, correction)[:, None, :] * sums["z"][None, :, None]
    first, last = sweep(west, east)
    again_w, again_e = beside(west_hot, last), beside(east_hot, first)
    return jnp.where(twice, again_w, west), jnp.where(twice, again_e, east)


def direct_extent(sums):
    return sums["extent_x"]


def body(divergence, neighbours, levels, sweeps):
    _, bx, nl, ny = divergence.shape
    modes = lax.axis_size("mode")
    columns = lax.axis_size("blk")
    nz = nl * modes
    nq = ny // modes
    jb = nz // columns
    fourier, weights, shift = fourier_table(ny)
    sx, lx = sine_table(bx)
    sz, lz = sine_table(nz)
    sl, ll = sine_table(nl)
    both = np.kron(sx, sl)
    to_global = sz @ np.kron(np.eye(modes), sl)
    rows = [r for d in range(1, modes) for r in (d * nl - 1, d * nl)]
    ends = f32(sz[rows])
    s0, s1 = f32(sx[0]), f32(sx[-1])
    e0, e1 = f32(sl[0]), f32(sl[-1])
    k = f32(shift)
    blk = lax.axis_index("blk")
    own_k = lax.dynamic_slice_in_dim(k, lax.axis_index("mode") * nq, nq)

    facts = jnp.concatenate([neighbours[0], levels, jnp.zeros((5,), jnp.int32)])
    facts = jnp.broadcast_to(facts.astype(jnp.float32)[None, :, None], (columns, 8, nq))
    s = jnp.left_shift(jnp.ones_like(levels), 2 * levels).astype(jnp.float32)[0]

    cells = divergence.reshape(bx * nl, ny)
    spectrum = jnp.dot(cells, f32(fourier.T), precision=HIGH)
    ghat = jnp.dot(f32(both), spectrum, precision=HIGH).reshape(bx, nl, ny)
    local = s * (f32(lx)[:, None, None] + f32(ll)[None, :, None]) + k
    vhat = ghat / local
    out = jnp.concatenate(
        [
            jnp.sum(vhat * e0[None, :, None], axis=1),
            jnp.sum(vhat * e1[None, :, None], axis=1),
            jnp.sum(vhat * s0[:, None, None], axis=0),
            jnp.sum(vhat * s1[:, None, None], axis=0),
        ]
    )
    out = jnp.stack([out[:, d * nq : (d + 1) * nq] for d in range(modes)])
    got = exchange(out, "mode", 0)
    vf, vl = got[:, :bx], got[:, bx : 2 * bx]
    a0 = got[:, 2 * bx : 2 * bx + nl].reshape(nz, nq)
    a1 = got[:, 2 * bx + nl :].reshape(nz, nq)
    jump = jnp.stack([t for d in range(1, modes) for t in (vf[d], vl[d - 1])])
    jump = jnp.einsum("rj,riq->ijq", ends, jump, precision=HIGHEST)
    whole = s * (f32(lx)[:, None, None] + f32(lz)[None, :, None]) + own_k
    lift = s * jump / whole
    m = f32(to_global)
    face0 = jnp.dot(m, a0, precision=HIGHEST) + jnp.sum(lift * s0[:, None, None], axis=0)
    face1 = jnp.dot(m, a1, precision=HIGHEST) + jnp.sum(lift * s1[:, None, None], axis=0)
    faces = [face0.reshape(columns, jb, nq), face1.reshape(columns, jb, nq), facts]
    faces = exchange(jnp.concatenate(faces, axis=1), "blk", 1)
    facts = faces[:, 2 * jb : 2 * jb + 3, 0].astype(jnp.int32)
    all_levels = facts[:, 2]
    level_ids = jnp.arange(sweeps.shape[0], dtype=jnp.int32)
    allowed = jnp.sum(jnp.where(all_levels[:, None] == level_ids, sweeps, 0), axis=1)
    all_s = jnp.left_shift(jnp.ones_like(all_levels), 2 * all_levels).astype(jnp.float32)

    own_lz = lax.dynamic_slice_in_dim(f32(lz), blk * jb, jb)
    sums = {
        "z": lax.dynamic_slice_in_dim(f32(sz.sum(axis=0)), blk * jb, jb),
        "perimeter": float(2 * nz + 2 * bx),
        "cells": float(bx * nz),
        "extent_z": float(nz),
        "extent_x": bx,
    }
    mu = own_lz[None, :, None] + own_k[None, None, :] / all_s[:, None, None]
    west, east = vcycle(faces[:, :jb], faces[:, jb : 2 * jb], facts[:, :2], mu, sums, all_s, allowed, own_k)
    back = exchange(jnp.concatenate([west, east], axis=1), "blk", 3)
    west, east = back[:, :jb].reshape(nz, nq), back[:, jb:].reshape(nz, nq)

    total = lift + s * (s0[:, None, None] * west + s1[:, None, None] * east) / whole
    inner = jnp.einsum("rj,ijq->riq", ends, total, precision=HIGHEST)
    none = jnp.zeros((bx, nq), jnp.float32)
    mt = f32(to_global.T)
    west = jnp.dot(mt, west, precision=HIGHEST).reshape(modes, nl, nq)
    east = jnp.dot(mt, east, precision=HIGHEST).reshape(modes, nl, nq)
    parcels = []
    for d in range(modes):
        below = none if d == 0 else inner[2 * d - 2] + vl[d - 1]
        above = none if d == modes - 1 else inner[2 * d + 1] + vf[d + 1]
        parcels.append(jnp.concatenate([below, above, west[d], east[d]]))
    got = exchange(jnp.stack(parcels), "mode", 4)
    got = jnp.concatenate([got[d] for d in range(modes)], axis=1)
    below, above = got[:bx], got[bx : 2 * bx]
    west, east = got[2 * bx : 2 * bx + nl], got[2 * bx + nl :]
    full = ghat + s * (
        s0[:, None, None] * west[None]
        + s1[:, None, None] * east[None]
        + e0[None, :, None] * below[:, None]
        + e1[None, :, None] * above[:, None]
    )
    full = (full / local).reshape(bx * nl, ny)
    cells = jnp.dot(f32(both), full, precision=HIGH)
    pressure = jnp.dot(cells, f32(weights[:, None] * fourier), precision=HIGH)
    return pressure.reshape(divergence.shape)


def solution(mesh):
    return jax.shard_map(
        body,
        mesh=mesh,
        in_specs=(P("blk", None, "mode", None), P("blk", None), P("blk"), P()),
        out_specs=P("blk", None, "mode", None),
        check_vma=False,
    )
```

```python
import functools

import jax
import jax.numpy as jnp
import numpy as np
from jax import lax
from jax.experimental import pallas as pl
from jax.experimental.pallas import tpu as pltpu
from jax.sharding import PartitionSpec as P

SWEEPS = 2
CITERS = 8
DAMPING = 0.8
HIGH = lax.Precision.HIGH
HIGHEST = lax.Precision.HIGHEST


def sine_table(extent):
    ordinal = np.arange(1, extent + 1)
    phases = np.outer(ordinal, ordinal) % (2 * (extent + 1))
    matrix = np.sqrt(2.0 / (extent + 1)) * np.sin(phases * (np.pi / (extent + 1)))
    eigen = 2.0 - 2.0 * np.cos(ordinal * (np.pi / (extent + 1)))
    return matrix, eigen


def fourier_table(length):
    half = length // 2
    ids = np.arange(length)
    wave = np.where(ids <= half, ids, ids - half)
    angles = (np.outer(wave, ids) % length) * (2.0 * np.pi / length)
    fourier = np.where((ids <= half)[:, None], np.cos(angles), np.sin(angles))
    weights = np.where((ids == 0) | (ids == half), 1.0, 2.0) / length
    shift = 2.0 - 2.0 * np.cos(wave * (2.0 * np.pi / length))
    return fourier, weights, shift


def f32(array):
    return jnp.asarray(np.asarray(array, np.float32))


def exchange_kernel(columns, n, src, dst, send_sem, recv_sem, own_sem):
    me = lax.axis_index("mode") * columns + lax.axis_index("blk")

    def place(slot):
        return {"mode": slot // columns, "blk": lax.rem(slot, columns)}

    def send(step):
        peer = lax.rem(me + step, n)
        return pltpu.make_async_remote_copy(
            src_ref=src.at[peer],
            dst_ref=dst.at[me],
            send_sem=send_sem.at[step],
            recv_sem=recv_sem.at[step],
            device_id=place(peer),
            device_id_type=pl.DeviceIdType.MESH,
        )

    barrier = pltpu.get_barrier_semaphore()

    @pl.loop(1, n)
    def _(step):
        pl.semaphore_signal(
            barrier,
            inc=1,
            device_id=place(lax.rem(me + step, n)),
            device_id_type=pl.DeviceIdType.MESH,
        )

    own = pltpu.make_async_copy(src.at[me], dst.at[me], own_sem)
    own.start()
    pl.semaphore_wait(barrier, n - 1)

    @pl.loop(1, n)
    def _(step):
        send(step).start()

    own.wait()

    @pl.loop(1, n)
    def _(step):
        send(step).wait()


def exchange(values, number):
    columns = lax.axis_size("blk")
    n = lax.axis_size("mode") * columns
    return pl.pallas_call(
        functools.partial(exchange_kernel, columns, n),
        out_shape=jax.ShapeDtypeStruct(values.shape, values.dtype),
        in_specs=[pl.BlockSpec(memory_space=pltpu.VMEM)],
        out_specs=pl.BlockSpec(memory_space=pltpu.VMEM),
        scratch_shapes=[
            pltpu.SemaphoreType.DMA((n,)),
            pltpu.SemaphoreType.DMA((n,)),
            pltpu.SemaphoreType.DMA,
        ],
        compiler_params=pltpu.CompilerParams(collective_id=number, has_side_effects=True),
        name=f"exchange_{number}",
    )(values)


def pack(rows, blocks):
    share = rows.shape[1] // blocks
    rows = rows.reshape(rows.shape[0], blocks, share).transpose(1, 0, 2)
    return rows.reshape(blocks, -1, 128)


def unpack(parcels, share):
    blocks = parcels.shape[0]
    rows = parcels.reshape(blocks, -1, share).transpose(1, 0, 2)
    return rows.reshape(-1, blocks * share)


def face_response(mu, extent):
    half = 0.5 * mu
    rho = 1.0 / (1.0 + half + jnp.sqrt(mu + half * half))
    rho2 = rho * rho
    power = jnp.ones_like(rho)
    base, left = rho, extent
    while left:
        if left & 1:
            power = power * base
        base, left = base * base, left >> 1
    scale = 1.0 / (1.0 - power * power * rho2)
    return rho * (1.0 - power * power) * scale, power * (1.0 - rho2) * scale


def vcycle(first_face, last_face, facts, mu, tables, allowed, stiffness, shift, share):
    lanes = first_face.shape[1]
    lane = jnp.arange(lanes, dtype=jnp.int32)
    slot, within = lane // share, lane % share
    same = within[:, None] == within[None, :]
    west_hot = (same & (slot[:, None] == facts[0][None, :])).astype(jnp.float32)
    east_hot = (same & (slot[:, None] == facts[1][None, :])).astype(jnp.float32)
    direct, across = face_response(mu, tables["bx"])
    twice = allowed > 1
    weight = tables["z"][:, None]

    def beside(hot, values):
        return jnp.dot(values, hot, precision=HIGHEST)

    def sweep(west, east):
        return (
            first_face + direct * west + across * east,
            last_face + across * west + direct * east,
        )

    used_w, used_e = beside(west_hot, last_face), beside(east_hot, first_face)
    second = sweep(used_w, used_e)
    first = jnp.where(twice, second[0], first_face)
    last = jnp.where(twice, second[1], last_face)
    west, east = beside(west_hot, last), beside(east_hot, first)
    change = west + east - jnp.where(twice, used_w + used_e, 0.0)
    rhs = jnp.sum(change * weight, axis=0) * stiffness
    diagonal = stiffness * tables["perimeter"] + tables["cells"] * shift
    coupling = stiffness * tables["nz"]
    link = west_hot + east_hot
    correction = DAMPING * rhs / diagonal
    for _ in range(CITERS - 1):
        linked = beside(link, correction[None])[0]
        correction = (
            correction + DAMPING * (rhs - diagonal * correction + coupling * linked) / diagonal
        )
    west = west + beside(west_hot, correction[None]) * weight
    east = east + beside(east_hot, correction[None]) * weight
    first, last = sweep(west, east)
    again_w, again_e = beside(west_hot, last), beside(east_hot, first)
    return jnp.where(twice, again_w, west), jnp.where(twice, again_e, east)


def middle(got, sweeps, k, bx, nl, modes, columns):
    nz = nl * modes
    share = k.shape[0] // (modes * columns)
    me = lax.axis_index("mode") * columns + lax.axis_index("blk")
    own_k = jnp.tile(lax.dynamic_slice_in_dim(k, me * share, share), columns)
    sx, lx = sine_table(bx)
    sz, lz = sine_table(nz)
    sl, _ = sine_table(nl)
    to_global = sz @ np.kron(np.eye(modes), sl)
    rows = [r for d in range(1, modes) for r in (d * nl - 1, d * nl)]
    ends = f32(sz[rows])
    s0, s1 = f32(sx[0]), f32(sx[-1])
    got = jnp.stack([unpack(got[d * columns : (d + 1) * columns], share) for d in range(modes)])
    lanes = got.shape[2]
    vf, vl = got[:, :bx], got[:, bx : 2 * bx]
    a0 = got[:, 2 * bx : 2 * bx + nl].reshape(nz, lanes)
    a1 = got[:, 2 * bx + nl : 2 * bx + 2 * nl].reshape(nz, lanes)
    facts = got[0, 2 * bx + 2 * nl : 2 * bx + 2 * nl + 3].astype(jnp.int32)
    level_ids = jnp.arange(sweeps.shape[0], dtype=jnp.int32)
    allowed = jnp.sum(jnp.where(facts[2][:, None] == level_ids, sweeps, 0), axis=1)
    s = jnp.left_shift(jnp.ones_like(facts[2]), 2 * facts[2]).astype(jnp.float32)

    jump = jnp.stack([t for d in range(1, modes) for t in (vf[d], vl[d - 1])])
    jump = jnp.einsum("rj,riq->ijq", ends, jump, precision=HIGHEST)
    ratio = own_k / s
    whole = f32(lx)[:, None, None] + f32(lz)[None, :, None] + ratio
    lift = jump / whole
    m = f32(to_global)
    face0 = jnp.dot(m, a0, precision=HIGHEST) + jnp.sum(lift * s0[:, None, None], axis=0)
    face1 = jnp.dot(m, a1, precision=HIGHEST) + jnp.sum(lift * s1[:, None, None], axis=0)
    tables = {
        "z": f32(sz.sum(axis=0)),
        "perimeter": float(2 * nz + 2 * bx),
        "cells": float(bx * nz),
        "nz": float(nz),
        "bx": bx,
    }
    mu = f32(lz)[:, None] + ratio[None, :]
    west, east = vcycle(face0, face1, facts, mu, tables, allowed, s, own_k, share)
    total = lift + (s0[:, None, None] * west + s1[:, None, None] * east) / whole
    inner = jnp.einsum("rj,ijq->riq", ends, total, precision=HIGHEST)
    none = jnp.zeros((bx, lanes), jnp.float32)
    mt = f32(to_global.T)
    west = jnp.dot(mt, west, precision=HIGHEST).reshape(modes, nl, lanes)
    east = jnp.dot(mt, east, precision=HIGHEST).reshape(modes, nl, lanes)
    parcels = []
    for d in range(modes):
        below = none if d == 0 else inner[2 * d - 2] + vl[d - 1]
        above = none if d == modes - 1 else inner[2 * d + 1] + vf[d + 1]
        parcels.append(pack(jnp.concatenate([below, above, west[d], east[d]]), columns))
    return jnp.concatenate(parcels)


def body(divergence, neighbours, levels, sweeps):
    _, bx, nl, ny = divergence.shape
    modes = lax.axis_size("mode")
    columns = lax.axis_size("blk")
    share = ny // (modes * columns)
    fourier, weights, shift = fourier_table(ny)
    sx, lx = sine_table(bx)
    sl, ll = sine_table(nl)
    both = np.kron(sx, sl)
    s0, s1 = f32(sx[0]), f32(sx[-1])
    e0, e1 = f32(sl[0]), f32(sl[-1])
    k = f32(shift)
    s = jnp.left_shift(jnp.ones_like(levels), 2 * levels).astype(jnp.float32)[0]

    cells = divergence.reshape(bx * nl, ny)
    spectrum = jnp.dot(cells, f32(fourier.T), precision=HIGH)
    ghat = jnp.dot(f32(both), spectrum, precision=HIGH).reshape(bx, nl, ny)
    local = s * (f32(lx)[:, None, None] + f32(ll)[None, :, None]) + k
    vhat = ghat / local
    per_row = 128 // share
    extra = -(2 * bx + 2 * nl + 3) % per_row + 3
    facts = jnp.concatenate([neighbours[0], levels, jnp.zeros((extra - 3,), jnp.int32)])
    out = [
        jnp.sum(vhat * e0[None, :, None], axis=1),
        jnp.sum(vhat * e1[None, :, None], axis=1),
        jnp.sum(vhat * s0[:, None, None], axis=0),
        jnp.sum(vhat * s1[:, None, None], axis=0),
        jnp.broadcast_to(facts.astype(jnp.float32)[:, None], (extra, ny)),
    ]
    got = exchange(pack(jnp.concatenate(out), modes * columns), 0)
    back = exchange(middle(got, sweeps, k, bx, nl, modes, columns), 1)
    got = unpack(back, share)
    below, above = got[:bx], got[bx : 2 * bx]
    west, east = got[2 * bx : 2 * bx + nl], got[2 * bx + nl :]
    full = ghat + s * (
        s0[:, None, None] * west[None]
        + s1[:, None, None] * east[None]
        + e0[None, :, None] * below[:, None]
        + e1[None, :, None] * above[:, None]
    )
    full = (full / local).reshape(bx * nl, ny)
    cells = jnp.dot(f32(both), full, precision=HIGH)
    pressure = jnp.dot(cells, f32(weights[:, None] * fourier), precision=HIGH)
    return pressure.reshape(divergence.shape)


def solution(mesh):
    return jax.shard_map(
        body,
        mesh=mesh,
        in_specs=(P("blk", None, "mode", None), P("blk", None), P("blk"), P()),
        out_specs=P("blk", None, "mode", None),
        check_vma=False,
    )
```

```python
import functools

import jax
import jax.numpy as jnp
import ml_dtypes
import numpy as np
from jax import lax
from jax.experimental import pallas as pl
from jax.experimental.pallas import tpu as pltpu
from jax.sharding import PartitionSpec as P

SWEEPS = 2
CITERS = 8
DAMPING = 0.8
HIGH = lax.Precision.HIGH
HIGHEST = lax.Precision.HIGHEST


def sine_table(extent):
    ordinal = np.arange(1, extent + 1)
    phases = np.outer(ordinal, ordinal) % (2 * (extent + 1))
    matrix = np.sqrt(2.0 / (extent + 1)) * np.sin(phases * (np.pi / (extent + 1)))
    eigen = 2.0 - 2.0 * np.cos(ordinal * (np.pi / (extent + 1)))
    return matrix, eigen


def fourier_table(length):
    half = length // 2
    ids = np.arange(length)
    wave = np.where(ids <= half, ids, ids - half)
    angles = (np.outer(wave, ids) % length) * (2.0 * np.pi / length)
    fourier = np.where((ids <= half)[:, None], np.cos(angles), np.sin(angles))
    weights = np.where((ids == 0) | (ids == half), 1.0, 2.0) / length
    shift = 2.0 - 2.0 * np.cos(wave * (2.0 * np.pi / length))
    return fourier, weights, shift


def f32(array):
    return jnp.asarray(np.asarray(array, np.float32))


def exchange_kernel(columns, n, src, dst, send_sem, recv_sem, own_sem):
    me = lax.axis_index("mode") * columns + lax.axis_index("blk")

    def place(slot):
        return {"mode": slot // columns, "blk": lax.rem(slot, columns)}

    def send(step):
        peer = lax.rem(me + step, n)
        return pltpu.make_async_remote_copy(
            src_ref=src.at[peer],
            dst_ref=dst.at[me],
            send_sem=send_sem.at[step],
            recv_sem=recv_sem.at[step],
            device_id=place(peer),
            device_id_type=pl.DeviceIdType.MESH,
        )

    barrier = pltpu.get_barrier_semaphore()

    @pl.loop(1, n)
    def _(step):
        pl.semaphore_signal(
            barrier,
            inc=1,
            device_id=place(lax.rem(me + step, n)),
            device_id_type=pl.DeviceIdType.MESH,
        )

    own = pltpu.make_async_copy(src.at[me], dst.at[me], own_sem)
    own.start()
    pl.semaphore_wait(barrier, n - 1)

    @pl.loop(1, n)
    def _(step):
        send(step).start()

    own.wait()

    @pl.loop(1, n)
    def _(step):
        send(step).wait()


def exchange(values, number):
    columns = lax.axis_size("blk")
    n = lax.axis_size("mode") * columns
    return pl.pallas_call(
        functools.partial(exchange_kernel, columns, n),
        out_shape=jax.ShapeDtypeStruct(values.shape, values.dtype),
        in_specs=[pl.BlockSpec(memory_space=pltpu.VMEM)],
        out_specs=pl.BlockSpec(memory_space=pltpu.VMEM),
        scratch_shapes=[
            pltpu.SemaphoreType.DMA((n,)),
            pltpu.SemaphoreType.DMA((n,)),
            pltpu.SemaphoreType.DMA,
        ],
        compiler_params=pltpu.CompilerParams(collective_id=number, has_side_effects=True),
        name=f"exchange_{number}",
    )(values)


def pack(rows, blocks):
    share = rows.shape[1] // blocks
    rows = rows.reshape(rows.shape[0], blocks, share).transpose(1, 0, 2)
    return rows.reshape(blocks, -1, 128)


def unpack(parcels, share):
    blocks = parcels.shape[0]
    rows = parcels.reshape(blocks, -1, share).transpose(1, 0, 2)
    return rows.reshape(-1, blocks * share)


def split(array):
    high = array.astype(jnp.bfloat16)
    return high, (array - high.astype(jnp.float32)).astype(jnp.bfloat16)


def split_table(array):
    array = np.asarray(array, np.float32)
    high = array.astype(ml_dtypes.bfloat16)
    low = (array - high.astype(np.float32)).astype(ml_dtypes.bfloat16)
    return jnp.asarray(high), jnp.asarray(low)


def dot3(a_high, a_low, b_high, b_low):
    def dot(a, b):
        return jnp.dot(a, b, preferred_element_type=jnp.float32)

    return dot(a_high, b_high) + (dot(a_high, b_low) + dot(a_low, b_high))


def inverse_of(value):
    guess = pl.reciprocal(value, approx=True)
    return guess * (2.0 - value * guess)


def parity_order(bx):
    return list(range(0, bx, 2)) + list(range(1, bx, 2))


def parity_tables(bx, nl):
    sx, _ = sine_table(bx)
    sl, _ = sine_table(nl)
    return [np.kron(sx[: bx // 2, part::2], sl) for part in (0, 1)]


def forward_kernel(bx, nl, lx, s0, x, fh, fl, kh, kl, lam, e0, e1, lane, vhat, rows, ah, al):
    half = bx // 2
    side = half * nl

    @pl.when(pl.program_id(0) == 0)
    def _():
        for c in range(half):
            top, bottom = x[0, c], x[0, bx - 1 - c]
            for part, value in ((0, top + bottom), (1, top - bottom)):
                high, low = split(value)
                ah[pl.ds((part * half + c) * nl, nl), :] = high
                al[pl.ds((part * half + c) * nl, nl), :] = low

    base = lam[...] + lane[0:1, :]
    scale = lane[1:2, :]
    sums = []
    for part in range(2):
        own = pl.ds(part * side, side)
        spectrum = dot3(ah[own, :], al[own, :], fh[...], fl[...])
        high, low = split(spectrum)
        ghat = dot3(kh[part], kl[part], high, low)
        total = None
        for c in range(half):
            i = part * half + c
            value = ghat[c * nl : (c + 1) * nl] * (scale * inverse_of(base + lx[i]))
            vhat[pl.ds(i * nl, nl), :] = value
            rows[pl.ds(i, 1), :] = jnp.sum(value * e0[...], axis=0, keepdims=True)
            rows[pl.ds(bx + i, 1), :] = jnp.sum(value * e1[...], axis=0, keepdims=True)
            term = value * s0[i]
            total = term if total is None else total + term
        sums.append(total)
    rows[pl.ds(2 * bx, nl), :] = sums[0] + sums[1]
    rows[pl.ds(2 * bx + nl, nl), :] = sums[0] - sums[1]


def inverse_kernel(bx, nl, lx, s0, tile, vhat, rows, fh, fl, kh, kl, lam, e0, e1, lane, out, uh, ul):
    half = bx // 2
    side = half * nl

    @pl.when(pl.program_id(0) == 0)
    def _():
        @pl.loop(0, vhat.shape[1] // tile)
        def _(step):
            q = pl.ds(pl.multiple_of(step * tile, tile), tile)
            base = lam[...] + lane[0:1, q]
            west, east = rows[pl.ds(2 * bx, nl), q], rows[pl.ds(2 * bx + nl, nl), q]
            for part in range(2):
                face = west + east if part == 0 else west - east
                parts = []
                for c in range(half):
                    i = part * half + c
                    load = (
                        face * s0[i] + rows[pl.ds(i, 1), q] * e0[...] + rows[pl.ds(bx + i, 1), q] * e1[...]
                    )
                    parts.append(vhat[pl.ds(i * nl, nl), q] + load * inverse_of(base + lx[i]))
                high, low = split(jnp.concatenate(parts))
                high, low = split(dot3(kh[part], kl[part], high, low))
                uh[pl.ds(part * side, side), q] = high
                ul[pl.ds(part * side, side), q] = low

    even = dot3(uh[pl.ds(0, side), :], ul[pl.ds(0, side), :], fh[...], fl[...])
    odd = dot3(uh[pl.ds(side, side), :], ul[pl.ds(side, side), :], fh[...], fl[...])
    for c in range(half):
        here = slice(c * nl, (c + 1) * nl)
        out[0, c] = even[here] + odd[here]
        out[0, bx - 1 - c] = even[here] - odd[here]


def local_tables(bx, nl):
    sx, lx = sine_table(bx)
    sl, ll = sine_table(nl)
    order = parity_order(bx)
    return (
        tuple(float(lx[i]) for i in order),
        tuple(float(sx[0, i]) for i in order),
        f32(ll[:, None]),
        f32(sl[0][:, None]),
        f32(sl[-1][:, None]),
    )


def whole_block(array):
    return pl.BlockSpec(array.shape, lambda t: (0,) * array.ndim)


LIMIT = 56 * 1024 * 1024


def forward(divergence, fourier, lane):
    _, bx, nl, ny = divergence.shape
    tile = min(256, ny)
    lx, s0, lam, e0, e1 = local_tables(bx, nl)
    even, odd = parity_tables(bx, nl)
    kh, kl = split_table(np.stack([even.T, odd.T]))
    fh, fl = split_table(fourier.T)
    across = pl.BlockSpec((ny, tile), lambda t: (0, t))
    cells = bx * nl
    count = 2 * bx + 2 * nl
    return pl.pallas_call(
        functools.partial(forward_kernel, bx, nl, lx, s0),
        grid=(ny // tile,),
        out_shape=[
            jax.ShapeDtypeStruct((cells, ny), jnp.float32),
            jax.ShapeDtypeStruct((count, ny), jnp.float32),
        ],
        in_specs=[whole_block(divergence), across, across]
        + [whole_block(a) for a in (kh, kl, lam, e0, e1)]
        + [pl.BlockSpec((8, tile), lambda t: (0, t))],
        out_specs=[
            pl.BlockSpec((cells, tile), lambda t: (0, t)),
            pl.BlockSpec((count, tile), lambda t: (0, t)),
        ],
        scratch_shapes=[pltpu.VMEM((cells, ny), jnp.bfloat16)] * 2,
        compiler_params=pltpu.CompilerParams(vmem_limit_bytes=LIMIT),
        name="forward",
    )(divergence, fh, fl, kh, kl, lam, e0, e1, lane)


def inverse(vhat, rows, weighted, lane, shape):
    _, bx, nl, ny = shape
    tile = min(256, ny)
    lx, s0, lam, e0, e1 = local_tables(bx, nl)
    even, odd = parity_tables(bx, nl)
    kh, kl = split_table(np.stack([even, odd]))
    fh, fl = split_table(weighted)
    across = pl.BlockSpec((ny, tile), lambda t: (0, t))
    cells = bx * nl
    return pl.pallas_call(
        functools.partial(inverse_kernel, bx, nl, lx, s0, tile),
        grid=(ny // tile,),
        out_shape=jax.ShapeDtypeStruct(shape, jnp.float32),
        in_specs=[whole_block(vhat), whole_block(rows), across, across]
        + [whole_block(a) for a in (kh, kl, lam, e0, e1, lane)],
        out_specs=pl.BlockSpec((1, bx, nl, tile), lambda t: (0, 0, 0, t)),
        scratch_shapes=[pltpu.VMEM((cells, ny), jnp.bfloat16)] * 2,
        compiler_params=pltpu.CompilerParams(vmem_limit_bytes=LIMIT),
        name="inverse",
    )(vhat, rows, fh, fl, kh, kl, lam, e0, e1, lane)


def face_response(mu, extent):
    half = 0.5 * mu
    rho = 1.0 / (1.0 + half + jnp.sqrt(mu + half * half))
    rho2 = rho * rho
    power = jnp.ones_like(rho)
    base, left = rho, extent
    while left:
        if left & 1:
            power = power * base
        base, left = base * base, left >> 1
    scale = 1.0 / (1.0 - power * power * rho2)
    return rho * (1.0 - power * power) * scale, power * (1.0 - rho2) * scale


def vcycle(first_face, last_face, facts, mu, tables, allowed, stiffness, shift, share):
    lanes = first_face.shape[1]
    lane = jnp.arange(lanes, dtype=jnp.int32)
    slot, within = lane // share, lane % share
    same = within[:, None] == within[None, :]
    west_hot = (same & (slot[:, None] == facts[0][None, :])).astype(jnp.float32)
    east_hot = (same & (slot[:, None] == facts[1][None, :])).astype(jnp.float32)
    direct, across = face_response(mu, tables["bx"])
    twice = allowed > 1
    weight = tables["z"][:, None]

    def beside(hot, values):
        return jnp.dot(values, hot, precision=HIGHEST)

    def sweep(west, east):
        return (
            first_face + direct * west + across * east,
            last_face + across * west + direct * east,
        )

    used_w, used_e = beside(west_hot, last_face), beside(east_hot, first_face)
    second = sweep(used_w, used_e)
    first = jnp.where(twice, second[0], first_face)
    last = jnp.where(twice, second[1], last_face)
    west, east = beside(west_hot, last), beside(east_hot, first)
    change = west + east - jnp.where(twice, used_w + used_e, 0.0)
    rhs = jnp.sum(change * weight, axis=0) * stiffness
    diagonal = stiffness * tables["perimeter"] + tables["cells"] * shift
    coupling = stiffness * tables["nz"]
    link = west_hot + east_hot
    correction = DAMPING * rhs / diagonal
    for _ in range(CITERS - 1):
        linked = beside(link, correction[None])[0]
        correction = (
            correction + DAMPING * (rhs - diagonal * correction + coupling * linked) / diagonal
        )
    west = west + beside(west_hot, correction[None]) * weight
    east = east + beside(east_hot, correction[None]) * weight
    first, last = sweep(west, east)
    again_w, again_e = beside(west_hot, last), beside(east_hot, first)
    return jnp.where(twice, again_w, west), jnp.where(twice, again_e, east)


def middle(got, sweeps, k, bx, nl, modes, columns):
    nz = nl * modes
    share = k.shape[0] // (modes * columns)
    me = lax.axis_index("mode") * columns + lax.axis_index("blk")
    own_k = jnp.tile(lax.dynamic_slice_in_dim(k, me * share, share), columns)
    sx, lx = sine_table(bx)
    sz, lz = sine_table(nz)
    sl, _ = sine_table(nl)
    to_global = sz @ np.kron(np.eye(modes), sl)
    rows = [r for d in range(1, modes) for r in (d * nl - 1, d * nl)]
    ends = f32(sz[rows])
    order = parity_order(bx)
    lx, s0, s1 = lx[order], f32(sx[0, order]), f32(sx[-1, order])
    got = jnp.stack([unpack(got[d * columns : (d + 1) * columns], share) for d in range(modes)])
    lanes = got.shape[2]
    vf, vl = got[:, :bx], got[:, bx : 2 * bx]
    a0 = got[:, 2 * bx : 2 * bx + nl].reshape(nz, lanes)
    a1 = got[:, 2 * bx + nl : 2 * bx + 2 * nl].reshape(nz, lanes)
    facts = got[0, 2 * bx + 2 * nl : 2 * bx + 2 * nl + 3].astype(jnp.int32)
    level_ids = jnp.arange(sweeps.shape[0], dtype=jnp.int32)
    allowed = jnp.sum(jnp.where(facts[2][:, None] == level_ids, sweeps, 0), axis=1)
    s = jnp.left_shift(jnp.ones_like(facts[2]), 2 * facts[2]).astype(jnp.float32)

    jump = jnp.stack([t for d in range(1, modes) for t in (vf[d], vl[d - 1])])
    jump = jnp.einsum("rj,riq->ijq", ends, jump, precision=HIGHEST)
    ratio = own_k / s
    whole = f32(lx)[:, None, None] + f32(lz)[None, :, None] + ratio
    lift = jump / whole
    m = f32(to_global)
    face0 = jnp.dot(m, a0, precision=HIGHEST) + jnp.sum(lift * s0[:, None, None], axis=0)
    face1 = jnp.dot(m, a1, precision=HIGHEST) + jnp.sum(lift * s1[:, None, None], axis=0)
    tables = {
        "z": f32(sz.sum(axis=0)),
        "perimeter": float(2 * nz + 2 * bx),
        "cells": float(bx * nz),
        "nz": float(nz),
        "bx": bx,
    }
    mu = f32(lz)[:, None] + ratio[None, :]
    west, east = vcycle(face0, face1, facts, mu, tables, allowed, s, own_k, share)
    total = lift + (s0[:, None, None] * west + s1[:, None, None] * east) / whole
    inner = jnp.einsum("rj,ijq->riq", ends, total, precision=HIGHEST)
    none = jnp.zeros((bx, lanes), jnp.float32)
    mt = f32(to_global.T)
    west = jnp.dot(mt, west, precision=HIGHEST).reshape(modes, nl, lanes)
    east = jnp.dot(mt, east, precision=HIGHEST).reshape(modes, nl, lanes)
    parcels = []
    for d in range(modes):
        below = none if d == 0 else inner[2 * d - 2] + vl[d - 1]
        above = none if d == modes - 1 else inner[2 * d + 1] + vf[d + 1]
        parcels.append(pack(jnp.concatenate([below, above, west[d], east[d]]), columns))
    return jnp.concatenate(parcels)


def body(divergence, neighbours, levels, sweeps):
    _, bx, nl, ny = divergence.shape
    modes = lax.axis_size("mode")
    columns = lax.axis_size("blk")
    share = ny // (modes * columns)
    fourier, weights, shift = fourier_table(ny)
    k = f32(shift)
    inv_s = jnp.right_shift(jnp.full_like(levels, 1 << 20), 2 * levels).astype(jnp.float32)[0]
    inv_s = inv_s * (0.5**20)
    lane = jnp.concatenate([(k * inv_s)[None], jnp.full((7, ny), inv_s)])
    vhat, out = forward(divergence, fourier, lane)
    per_row = 128 // share
    extra = -(2 * bx + 2 * nl + 3) % per_row + 3
    facts = jnp.concatenate([neighbours[0], levels, jnp.zeros((extra - 3,), jnp.int32)])
    facts = jnp.broadcast_to(facts.astype(jnp.float32)[:, None], (extra, ny))
    out = jnp.concatenate([out, facts])
    got = exchange(pack(out, modes * columns), 0)
    back = exchange(middle(got, sweeps, k, bx, nl, modes, columns), 1)
    return inverse(vhat, unpack(back, share), weights[:, None] * fourier, lane, divergence.shape)


def solution(mesh):
    return jax.shard_map(
        body,
        mesh=mesh,
        in_specs=(P("blk", None, "mode", None), P("blk", None), P("blk"), P()),
        out_specs=P("blk", None, "mode", None),
        check_vma=False,
    )
```

```python
import functools

import jax
import jax.numpy as jnp
import ml_dtypes
import numpy as np
from jax import lax
from jax.experimental import pallas as pl
from jax.experimental.pallas import tpu as pltpu
from jax.sharding import PartitionSpec as P

SWEEPS = 2
CITERS = 8
DAMPING = 0.8


def sine_table(extent):
    ordinal = np.arange(1, extent + 1)
    phases = np.outer(ordinal, ordinal) % (2 * (extent + 1))
    matrix = np.sqrt(2.0 / (extent + 1)) * np.sin(phases * (np.pi / (extent + 1)))
    eigen = 2.0 - 2.0 * np.cos(ordinal * (np.pi / (extent + 1)))
    return matrix, eigen


def fourier_table(length):
    half = length // 2
    ids = np.arange(length)
    wave = np.where(ids <= half, ids, ids - half)
    angles = (np.outer(wave, ids) % length) * (2.0 * np.pi / length)
    fourier = np.where((ids <= half)[:, None], np.cos(angles), np.sin(angles))
    weights = np.where((ids == 0) | (ids == half), 1.0, 2.0) / length
    shift = 2.0 - 2.0 * np.cos(wave * (2.0 * np.pi / length))
    return fourier, weights, shift


def f32(array):
    return jnp.asarray(np.asarray(array, np.float32))


def exchange_kernel(columns, n, src, dst, send_sem, recv_sem, own_sem):
    me = lax.axis_index("mode") * columns + lax.axis_index("blk")

    def place(slot):
        return {"mode": slot // columns, "blk": lax.rem(slot, columns)}

    def send(step):
        peer = lax.rem(me + step, n)
        return pltpu.make_async_remote_copy(
            src_ref=src.at[peer],
            dst_ref=dst.at[me],
            send_sem=send_sem.at[step],
            recv_sem=recv_sem.at[step],
            device_id=place(peer),
            device_id_type=pl.DeviceIdType.MESH,
        )

    barrier = pltpu.get_barrier_semaphore()

    @pl.loop(1, n)
    def _(step):
        pl.semaphore_signal(
            barrier,
            inc=1,
            device_id=place(lax.rem(me + step, n)),
            device_id_type=pl.DeviceIdType.MESH,
        )

    own = pltpu.make_async_copy(src.at[me], dst.at[me], own_sem)
    own.start()
    pl.semaphore_wait(barrier, n - 1)

    @pl.loop(1, n)
    def _(step):
        send(step).start()

    own.wait()

    @pl.loop(1, n)
    def _(step):
        send(step).wait()


def exchange(values, number):
    columns = lax.axis_size("blk")
    n = lax.axis_size("mode") * columns
    return pl.pallas_call(
        functools.partial(exchange_kernel, columns, n),
        out_shape=jax.ShapeDtypeStruct(values.shape, values.dtype),
        in_specs=[pl.BlockSpec(memory_space=pltpu.VMEM)],
        out_specs=pl.BlockSpec(memory_space=pltpu.VMEM),
        scratch_shapes=[
            pltpu.SemaphoreType.DMA((n,)),
            pltpu.SemaphoreType.DMA((n,)),
            pltpu.SemaphoreType.DMA,
        ],
        compiler_params=pltpu.CompilerParams(collective_id=number, has_side_effects=True),
        name=f"exchange_{number}",
    )(values)


def pack(rows, blocks):
    share = rows.shape[1] // blocks
    rows = rows.reshape(rows.shape[0], blocks, share).transpose(1, 0, 2)
    return rows.reshape(blocks, -1, 128)


def unpack(parcels, share):
    blocks = parcels.shape[0]
    rows = parcels.reshape(blocks, -1, share).transpose(1, 0, 2)
    return rows.reshape(-1, blocks * share)


def split(array):
    high = array.astype(jnp.bfloat16)
    return high, (array - high.astype(jnp.float32)).astype(jnp.bfloat16)


def split_table(array):
    array = np.asarray(array, np.float32)
    high = array.astype(ml_dtypes.bfloat16)
    low = (array - high.astype(np.float32)).astype(ml_dtypes.bfloat16)
    return jnp.asarray(high), jnp.asarray(low)


def dot3(a_high, a_low, b_high, b_low):
    def dot(a, b):
        return jnp.dot(a, b, preferred_element_type=jnp.float32)

    return dot(a_high, b_high) + (dot(a_high, b_low) + dot(a_low, b_high))


def inverse_of(value):
    guess = pl.reciprocal(value, approx=True)
    return guess * (2.0 - value * guess)


def parity_order(bx):
    return list(range(0, bx, 2)) + list(range(1, bx, 2))


def parity_tables(bx, nl):
    sx, _ = sine_table(bx)
    sl, _ = sine_table(nl)
    return [np.kron(sx[: bx // 2, part::2], sl) for part in (0, 1)]


def forward_kernel(bx, nl, lx, s0, x, fh, fl, kh, kl, lam, e0, e1, lane, vhat, rows, ah, al):
    half = bx // 2
    side = half * nl

    @pl.when(pl.program_id(0) == 0)
    def _():
        for c in range(half):
            top, bottom = x[0, c], x[0, bx - 1 - c]
            for part, value in ((0, top + bottom), (1, top - bottom)):
                high, low = split(value)
                ah[pl.ds((part * half + c) * nl, nl), :] = high
                al[pl.ds((part * half + c) * nl, nl), :] = low

    base = lam[...] + lane[0:1, :]
    scale = lane[1:2, :]
    sums = []
    for part in range(2):
        own = pl.ds(part * side, side)
        spectrum = dot3(ah[own, :], al[own, :], fh[...], fl[...])
        high, low = split(spectrum)
        ghat = dot3(kh[part], kl[part], high, low)
        total = None
        for c in range(half):
            i = part * half + c
            value = ghat[c * nl : (c + 1) * nl] * (scale * inverse_of(base + lx[i]))
            vhat[pl.ds(i * nl, nl), :] = value
            rows[pl.ds(i, 1), :] = jnp.sum(value * e0[...], axis=0, keepdims=True)
            rows[pl.ds(bx + i, 1), :] = jnp.sum(value * e1[...], axis=0, keepdims=True)
            term = value * s0[i]
            total = term if total is None else total + term
        sums.append(total)
    rows[pl.ds(2 * bx, nl), :] = sums[0] + sums[1]
    rows[pl.ds(2 * bx + nl, nl), :] = sums[0] - sums[1]


def inverse_kernel(bx, nl, lx, s0, tile, vhat, rows, fh, fl, kh, kl, lam, e0, e1, lane, out, uh, ul):
    half = bx // 2
    side = half * nl

    @pl.when(pl.program_id(0) == 0)
    def _():
        @pl.loop(0, vhat.shape[1] // tile)
        def _(step):
            q = pl.ds(pl.multiple_of(step * tile, tile), tile)
            base = lam[...] + lane[0:1, q]
            west, east = rows[pl.ds(2 * bx, nl), q], rows[pl.ds(2 * bx + nl, nl), q]
            for part in range(2):
                face = west + east if part == 0 else west - east
                parts = []
                for c in range(half):
                    i = part * half + c
                    load = (
                        face * s0[i] + rows[pl.ds(i, 1), q] * e0[...] + rows[pl.ds(bx + i, 1), q] * e1[...]
                    )
                    parts.append(vhat[pl.ds(i * nl, nl), q] + load * inverse_of(base + lx[i]))
                high, low = split(jnp.concatenate(parts))
                high, low = split(dot3(kh[part], kl[part], high, low))
                uh[pl.ds(part * side, side), q] = high
                ul[pl.ds(part * side, side), q] = low

    even = dot3(uh[pl.ds(0, side), :], ul[pl.ds(0, side), :], fh[...], fl[...])
    odd = dot3(uh[pl.ds(side, side), :], ul[pl.ds(side, side), :], fh[...], fl[...])
    for c in range(half):
        here = slice(c * nl, (c + 1) * nl)
        out[0, c] = even[here] + odd[here]
        out[0, bx - 1 - c] = even[here] - odd[here]


def local_tables(bx, nl):
    sx, lx = sine_table(bx)
    sl, ll = sine_table(nl)
    order = parity_order(bx)
    return (
        tuple(float(lx[i]) for i in order),
        tuple(float(sx[0, i]) for i in order),
        f32(ll[:, None]),
        f32(sl[0][:, None]),
        f32(sl[-1][:, None]),
    )


def whole_block(array):
    return pl.BlockSpec(array.shape, lambda t: (0,) * array.ndim)


LIMIT = 56 * 1024 * 1024


def forward(divergence, fourier, lane):
    _, bx, nl, ny = divergence.shape
    tile = min(256, ny)
    lx, s0, lam, e0, e1 = local_tables(bx, nl)
    even, odd = parity_tables(bx, nl)
    kh, kl = split_table(np.stack([even.T, odd.T]))
    fh, fl = split_table(fourier.T)
    across = pl.BlockSpec((ny, tile), lambda t: (0, t))
    cells = bx * nl
    count = 2 * bx + 2 * nl
    return pl.pallas_call(
        functools.partial(forward_kernel, bx, nl, lx, s0),
        grid=(ny // tile,),
        out_shape=[
            jax.ShapeDtypeStruct((cells, ny), jnp.float32),
            jax.ShapeDtypeStruct((count, ny), jnp.float32),
        ],
        in_specs=[whole_block(divergence), across, across]
        + [whole_block(a) for a in (kh, kl, lam, e0, e1)]
        + [pl.BlockSpec((8, tile), lambda t: (0, t))],
        out_specs=[
            pl.BlockSpec((cells, tile), lambda t: (0, t)),
            pl.BlockSpec((count, tile), lambda t: (0, t)),
        ],
        scratch_shapes=[pltpu.VMEM((cells, ny), jnp.bfloat16)] * 2,
        compiler_params=pltpu.CompilerParams(vmem_limit_bytes=LIMIT),
        name="forward",
    )(divergence, fh, fl, kh, kl, lam, e0, e1, lane)


def inverse(vhat, rows, weighted, lane, shape):
    _, bx, nl, ny = shape
    tile = min(256, ny)
    lx, s0, lam, e0, e1 = local_tables(bx, nl)
    even, odd = parity_tables(bx, nl)
    kh, kl = split_table(np.stack([even, odd]))
    fh, fl = split_table(weighted)
    across = pl.BlockSpec((ny, tile), lambda t: (0, t))
    cells = bx * nl
    return pl.pallas_call(
        functools.partial(inverse_kernel, bx, nl, lx, s0, tile),
        grid=(ny // tile,),
        out_shape=jax.ShapeDtypeStruct(shape, jnp.float32),
        in_specs=[whole_block(vhat), whole_block(rows), across, across]
        + [whole_block(a) for a in (kh, kl, lam, e0, e1, lane)],
        out_specs=pl.BlockSpec((1, bx, nl, tile), lambda t: (0, 0, 0, t)),
        scratch_shapes=[pltpu.VMEM((cells, ny), jnp.bfloat16)] * 2,
        compiler_params=pltpu.CompilerParams(vmem_limit_bytes=LIMIT),
        name="inverse",
    )(vhat, rows, fh, fl, kh, kl, lam, e0, e1, lane)


def face_response(mu, extent):
    half = 0.5 * mu
    rho = 1.0 / (1.0 + half + jnp.sqrt(mu + half * half))
    rho2 = rho * rho
    power = jnp.ones_like(rho)
    base, left = rho, extent
    while left:
        if left & 1:
            power = power * base
        base, left = base * base, left >> 1
    scale = 1.0 / (1.0 - power * power * rho2)
    return rho * (1.0 - power * power) * scale, power * (1.0 - rho2) * scale


def split3(array):
    high, low = split(array)
    rest = array - high.astype(jnp.float32) - low.astype(jnp.float32)
    return high, low, rest.astype(jnp.bfloat16)


def moved(values, hot):
    first, second, third = (
        jnp.dot(part, hot, preferred_element_type=jnp.float32) for part in split3(values)
    )
    return first + (second + third)


def middle_kernel(
    bx, nz, lx, s0, jump, a0, a1, rows, slots, lift_table, end_h, end_l, to_h, to_l, from_h, from_l,
    lz, zsum, west_out, east_out, inner, lift,
):
    half = bx // 2
    lanes = a0.shape[1]
    west_slot, east_slot = rows[0:1, :], rows[1:2, :]
    stiffness, twice = rows[2:3, :], rows[3:4, :] > 0.5
    shift, ratio = rows[4:5, :], rows[5:6, :]
    mu = lz[...] + ratio
    lift_rows = lift_table[...]

    sums = []
    for part in range(2):
        total = jnp.zeros((nz, lanes), jnp.float32)
        for c in range(half):
            i = part * half + c
            high, low = split(jump[i])
            both = jnp.concatenate([high, low, high])
            value = jnp.dot(lift_rows, both, preferred_element_type=jnp.float32)
            value = value * inverse_of(mu + lx[i])
            lift[i] = value
            total = total + s0[i] * value
        sums.append(total)
    first_face = dot3(to_h[...], to_l[...], *split(a0[...])) + sums[0] + sums[1]
    last_face = dot3(to_h[...], to_l[...], *split(a1[...])) + sums[0] - sums[1]

    west_hot = jnp.where(slots[...] == west_slot, 1.0, 0.0)
    east_hot = jnp.where(slots[...] == east_slot, 1.0, 0.0)
    link = (west_hot + east_hot).astype(jnp.bfloat16)
    west_hot, east_hot = west_hot.astype(jnp.bfloat16), east_hot.astype(jnp.bfloat16)
    direct, across = face_response(mu, bx)
    weight = zsum[...]

    def sweep(west, east):
        return (
            first_face + direct * west + across * east,
            last_face + across * west + direct * east,
        )

    used_w, used_e = moved(last_face, west_hot), moved(first_face, east_hot)
    second = sweep(used_w, used_e)
    first = jnp.where(twice, second[0], first_face)
    last = jnp.where(twice, second[1], last_face)
    west, east = moved(last, west_hot), moved(first, east_hot)
    change = west + east - jnp.where(twice, used_w + used_e, 0.0)
    rhs = jnp.sum(change * weight, axis=0, keepdims=True) * stiffness
    diagonal = stiffness * float(2 * nz + 2 * bx) + float(bx * nz) * shift
    coupling = stiffness * float(nz)
    spread = jnp.zeros((16, lanes), jnp.float32)
    rhs, diagonal, coupling = rhs + spread, diagonal + spread, coupling + spread
    step = DAMPING / diagonal
    correction = step * rhs
    for _ in range(CITERS - 1):
        linked = moved(correction, link)
        correction = correction + step * (rhs - diagonal * correction + coupling * linked)
    west = west + moved(correction, west_hot)[0:1] * weight
    east = east + moved(correction, east_hot)[0:1] * weight
    first, last = sweep(west, east)
    west = jnp.where(twice, moved(last, west_hot), west)
    east = jnp.where(twice, moved(first, east_hot), east)

    west_out[...] = dot3(from_h[...], from_l[...], *split(west))
    east_out[...] = dot3(from_h[...], from_l[...], *split(east))
    for part in range(2):
        face = west + east if part == 0 else west - east
        for c in range(half):
            i = part * half + c
            total = lift[i] + (s0[i] * face) * inverse_of(mu + lx[i])
            inner[i] = dot3(end_h[...], end_l[...], *split(total))


def middle(got, sweeps, k, bx, nl, modes, columns):
    nz = nl * modes
    share = k.shape[0] // (modes * columns)
    me = lax.axis_index("mode") * columns + lax.axis_index("blk")
    own_k = jnp.tile(lax.dynamic_slice_in_dim(k, me * share, share), columns)
    sx, lx = sine_table(bx)
    sz, lz = sine_table(nz)
    sl, _ = sine_table(nl)
    to_global = sz @ np.kron(np.eye(modes), sl)
    picks = [r for d in range(1, modes) for r in (d * nl - 1, d * nl)]
    order = parity_order(bx)
    ends = np.zeros((-(-len(picks) // 16) * 16, nz))
    ends[: len(picks)] = sz[picks]
    end_h, end_l = split_table(ends)
    to_h, to_l = split_table(to_global)
    from_h, from_l = split_table(to_global.T)
    lift_table = jnp.concatenate([end_h.T, end_h.T, end_l.T], axis=1)
    got = jnp.stack([unpack(got[d * columns : (d + 1) * columns], share) for d in range(modes)])
    lanes = got.shape[2]
    vf, vl = got[:, :bx], got[:, bx : 2 * bx]
    a0 = got[:, 2 * bx : 2 * bx + nl].reshape(nz, lanes)
    a1 = got[:, 2 * bx + nl : 2 * bx + 2 * nl].reshape(nz, lanes)
    facts = got[0, 2 * bx + 2 * nl : 2 * bx + 2 * nl + 3]
    level = facts[2].astype(jnp.int32)
    level_ids = jnp.arange(sweeps.shape[0], dtype=jnp.int32)
    allowed = jnp.sum(jnp.where(level[:, None] == level_ids, sweeps, 0), axis=1)
    s = jnp.left_shift(jnp.ones_like(level), 2 * level).astype(jnp.float32)
    twice = (allowed > 1).astype(jnp.float32)
    rows = jnp.stack([facts[0], facts[1], s, twice, own_k, own_k / s, s, s])
    slot, within = np.arange(lanes) // share, np.arange(lanes) % share
    slots = f32(np.where(within[:, None] == within[None, :], slot[:, None], -2))
    jump = [t for d in range(1, modes) for t in (vf[d], vl[d - 1])]
    jump += [jnp.zeros_like(vf[0])] * (ends.shape[0] - len(picks))
    jump = jnp.stack(jump, axis=1)
    west, east, inner = pl.pallas_call(
        functools.partial(
            middle_kernel,
            bx,
            nz,
            tuple(float(lx[i]) for i in order),
            tuple(float(sx[0, i]) for i in order),
        ),
        out_shape=[
            jax.ShapeDtypeStruct((nz, lanes), jnp.float32),
            jax.ShapeDtypeStruct((nz, lanes), jnp.float32),
            jax.ShapeDtypeStruct((bx, ends.shape[0], lanes), jnp.float32),
        ],
        in_specs=[pl.BlockSpec(memory_space=pltpu.VMEM)] * 14,
        out_specs=[pl.BlockSpec(memory_space=pltpu.VMEM)] * 3,
        scratch_shapes=[pltpu.VMEM((bx, nz, lanes), jnp.float32)],
        compiler_params=pltpu.CompilerParams(vmem_limit_bytes=32 * 1024 * 1024),
        name="middle",
    )(
        jump, a0, a1, rows, slots, lift_table, end_h, end_l, to_h, to_l, from_h, from_l,
        f32(lz[:, None]), f32(sz.sum(axis=0)[:, None]),
    )
    west, east = west.reshape(modes, nl, lanes), east.reshape(modes, nl, lanes)
    none = jnp.zeros((bx, lanes), jnp.float32)
    parcels = []
    for d in range(modes):
        below = none if d == 0 else inner[:, 2 * d - 2] + vl[d - 1]
        above = none if d == modes - 1 else inner[:, 2 * d + 1] + vf[d + 1]
        parcels.append(pack(jnp.concatenate([below, above, west[d], east[d]]), columns))
    return jnp.concatenate(parcels)


def body(divergence, neighbours, levels, sweeps):
    _, bx, nl, ny = divergence.shape
    modes = lax.axis_size("mode")
    columns = lax.axis_size("blk")
    share = ny // (modes * columns)
    fourier, weights, shift = fourier_table(ny)
    k = f32(shift)
    inv_s = jnp.right_shift(jnp.full_like(levels, 1 << 20), 2 * levels).astype(jnp.float32)[0]
    inv_s = inv_s * (0.5**20)
    lane = jnp.concatenate([(k * inv_s)[None], jnp.full((7, ny), inv_s)])
    vhat, out = forward(divergence, fourier, lane)
    per_row = 128 // share
    extra = -(2 * bx + 2 * nl + 3) % per_row + 3
    facts = jnp.concatenate([neighbours[0], levels, jnp.zeros((extra - 3,), jnp.int32)])
    facts = jnp.broadcast_to(facts.astype(jnp.float32)[:, None], (extra, ny))
    out = jnp.concatenate([out, facts])
    got = exchange(pack(out, modes * columns), 0)
    back = exchange(middle(got, sweeps, k, bx, nl, modes, columns), 1)
    return inverse(vhat, unpack(back, share), weights[:, None] * fourier, lane, divergence.shape)


def solution(mesh):
    return jax.shard_map(
        body,
        mesh=mesh,
        in_specs=(P("blk", None, "mode", None), P("blk", None), P("blk"), P()),
        out_specs=P("blk", None, "mode", None),
        check_vma=False,
    )
```

```python
import functools

import jax
import jax.numpy as jnp
import ml_dtypes
import numpy as np
from jax import lax
from jax.experimental import pallas as pl
from jax.experimental.pallas import tpu as pltpu
from jax.sharding import PartitionSpec as P

SWEEPS = 2
CITERS = 8
DAMPING = 0.8


def sine_table(extent):
    ordinal = np.arange(1, extent + 1)
    phases = np.outer(ordinal, ordinal) % (2 * (extent + 1))
    matrix = np.sqrt(2.0 / (extent + 1)) * np.sin(phases * (np.pi / (extent + 1)))
    eigen = 2.0 - 2.0 * np.cos(ordinal * (np.pi / (extent + 1)))
    return matrix, eigen


def fourier_table(length):
    half = length // 2
    ids = np.arange(length)
    wave = np.where(ids <= half, ids, ids - half)
    angles = (np.outer(wave, ids) % length) * (2.0 * np.pi / length)
    fourier = np.where((ids <= half)[:, None], np.cos(angles), np.sin(angles))
    weights = np.where((ids == 0) | (ids == half), 1.0, 2.0) / length
    shift = 2.0 - 2.0 * np.cos(wave * (2.0 * np.pi / length))
    return fourier, weights, shift


def f32(array):
    return jnp.asarray(np.asarray(array, np.float32))


def exchange_kernel(columns, n, src, dst, send_sem, recv_sem, own_sem):
    me = lax.axis_index("mode") * columns + lax.axis_index("blk")

    def place(slot):
        return {"mode": slot // columns, "blk": lax.rem(slot, columns)}

    def send(step):
        peer = lax.rem(me + step, n)
        return pltpu.make_async_remote_copy(
            src_ref=src.at[peer],
            dst_ref=dst.at[me],
            send_sem=send_sem.at[step],
            recv_sem=recv_sem.at[step],
            device_id=place(peer),
            device_id_type=pl.DeviceIdType.MESH,
        )

    barrier = pltpu.get_barrier_semaphore()

    @pl.loop(1, n)
    def _(step):
        pl.semaphore_signal(
            barrier,
            inc=1,
            device_id=place(lax.rem(me + step, n)),
            device_id_type=pl.DeviceIdType.MESH,
        )

    own = pltpu.make_async_copy(src.at[me], dst.at[me], own_sem)
    own.start()
    pl.semaphore_wait(barrier, n - 1)

    @pl.loop(1, n)
    def _(step):
        send(step).start()

    own.wait()

    @pl.loop(1, n)
    def _(step):
        send(step).wait()


def exchange(values, number):
    columns = lax.axis_size("blk")
    n = lax.axis_size("mode") * columns
    return pl.pallas_call(
        functools.partial(exchange_kernel, columns, n),
        out_shape=jax.ShapeDtypeStruct(values.shape, values.dtype),
        in_specs=[pl.BlockSpec(memory_space=pltpu.VMEM)],
        out_specs=pl.BlockSpec(memory_space=pltpu.VMEM),
        scratch_shapes=[
            pltpu.SemaphoreType.DMA((n,)),
            pltpu.SemaphoreType.DMA((n,)),
            pltpu.SemaphoreType.DMA,
        ],
        compiler_params=pltpu.CompilerParams(collective_id=number, has_side_effects=True),
        name=f"exchange_{number}",
    )(values)


def pack(rows, blocks):
    share = rows.shape[1] // blocks
    rows = rows.reshape(rows.shape[0], blocks, share).transpose(1, 0, 2)
    return rows.reshape(blocks, -1, 128)


def unpack(parcels, share):
    blocks = parcels.shape[0]
    rows = parcels.reshape(blocks, -1, share).transpose(1, 0, 2)
    return rows.reshape(-1, blocks * share)


def split(array):
    high = array.astype(jnp.bfloat16)
    return high, (array - high.astype(jnp.float32)).astype(jnp.bfloat16)


def split_table(array):
    array = np.asarray(array, np.float32)
    high = array.astype(ml_dtypes.bfloat16)
    low = (array - high.astype(np.float32)).astype(ml_dtypes.bfloat16)
    return jnp.asarray(high), jnp.asarray(low)


def dot3(a_high, a_low, b_high, b_low):
    def dot(a, b):
        return jnp.dot(a, b, preferred_element_type=jnp.float32)

    return dot(a_high, b_high) + (dot(a_high, b_low) + dot(a_low, b_high))


def inverse_of(value):
    guess = pl.reciprocal(value, approx=True)
    return guess * (2.0 - value * guess)


def parity_order(bx):
    return list(range(0, bx, 2)) + list(range(1, bx, 2))


def parity_tables(bx, nl):
    sx, _ = sine_table(bx)
    sl, _ = sine_table(nl)
    return [np.kron(sx[: bx // 2, part::2], sl) for part in (0, 1)]


def forward_kernel(bx, nl, lx, s0, x, fh, fl, kh, kl, lam, e0, e1, lane, facts, vhat, *rest):
    parcels, rows, ah, al = rest if len(rest) == 4 else (None,) + rest
    half = bx // 2
    side = half * nl

    @pl.when(pl.program_id(0) == 0)
    def _():
        for c in range(half):
            top, bottom = x[0, c], x[0, bx - 1 - c]
            for part, value in ((0, top + bottom), (1, top - bottom)):
                high, low = split(value)
                ah[pl.ds((part * half + c) * nl, nl), :] = high
                al[pl.ds((part * half + c) * nl, nl), :] = low

    base = lam[...] + lane[0:1, :]
    scale = lane[1:2, :]
    sums = []
    for part in range(2):
        own = pl.ds(part * side, side)
        spectrum = dot3(ah[own, :], al[own, :], fh[...], fl[...])
        high, low = split(spectrum)
        ghat = dot3(kh[part], kl[part], high, low)
        total = None
        for c in range(half):
            i = part * half + c
            value = ghat[c * nl : (c + 1) * nl] * (scale * inverse_of(base + lx[i]))
            vhat[pl.ds(i * nl, nl), :] = value
            rows[pl.ds(i, 1), :] = jnp.sum(value * e0[...], axis=0, keepdims=True)
            rows[pl.ds(bx + i, 1), :] = jnp.sum(value * e1[...], axis=0, keepdims=True)
            term = value * s0[i]
            total = term if total is None else total + term
        sums.append(total)
    rows[pl.ds(2 * bx, nl), :] = sums[0] + sums[1]
    rows[pl.ds(2 * bx + nl, nl), :] = sums[0] - sums[1]
    if parcels is not None:
        for h in range(parcels.shape[0] // 4):
            here = pl.ds(h * 128, 128)
            groups = lane_groups([rows[pl.ds(g * bx, bx), here] for g in range(4)])
            for c in range(4):
                parcels[h * 4 + c, pl.ds(0, bx), :] = groups[c]
                parcels[h * 4 + c, pl.ds(bx, 8), :] = facts[...]


def inverse_kernel(bx, nl, lx, s0, tile, vhat, got, fh, fl, kh, kl, lam, e0, e1, lane, out, uh, ul, *rest):
    rows = rest[0] if rest else got
    half = bx // 2
    side = half * nl

    @pl.when(pl.program_id(0) == 0)
    def _():
        if rest:
            for h in range(got.shape[0] // 4):
                groups = lane_groups([got[h * 4 + c] for c in range(4)])
                for g in range(4):
                    rows[pl.ds(g * bx, bx), pl.ds(h * 128, 128)] = groups[g]

        @pl.loop(0, vhat.shape[1] // tile)
        def _(step):
            q = pl.ds(pl.multiple_of(step * tile, tile), tile)
            base = lam[...] + lane[0:1, q]
            west, east = rows[pl.ds(2 * bx, nl), q], rows[pl.ds(2 * bx + nl, nl), q]
            for part in range(2):
                face = west + east if part == 0 else west - east
                parts = []
                for c in range(half):
                    i = part * half + c
                    load = (
                        face * s0[i] + rows[pl.ds(i, 1), q] * e0[...] + rows[pl.ds(bx + i, 1), q] * e1[...]
                    )
                    parts.append(vhat[pl.ds(i * nl, nl), q] + load * inverse_of(base + lx[i]))
                high, low = split(jnp.concatenate(parts))
                high, low = split(dot3(kh[part], kl[part], high, low))
                uh[pl.ds(part * side, side), q] = high
                ul[pl.ds(part * side, side), q] = low

    even = dot3(uh[pl.ds(0, side), :], ul[pl.ds(0, side), :], fh[...], fl[...])
    odd = dot3(uh[pl.ds(side, side), :], ul[pl.ds(side, side), :], fh[...], fl[...])
    for c in range(half):
        here = slice(c * nl, (c + 1) * nl)
        out[0, c] = even[here] + odd[here]
        out[0, bx - 1 - c] = even[here] - odd[here]


def local_tables(bx, nl, tile):
    sx, lx = sine_table(bx)
    sl, ll = sine_table(nl)
    order = parity_order(bx)
    return (
        tuple(float(lx[i]) for i in order),
        tuple(float(sx[0, i]) for i in order),
        f32(np.tile(ll[:, None], (1, tile))),
        f32(np.tile(sl[0][:, None], (1, tile))),
        f32(np.tile(sl[-1][:, None], (1, tile))),
    )


def lane_groups(arrays):
    count = len(arrays)
    width = 128 // count
    group = lax.broadcasted_iota(jnp.int32, arrays[0].shape, 1)
    results = []
    for k in range(count):
        result = arrays[k]
        for j in range(count):
            if j != k:
                turned = pltpu.roll(arrays[j], (j - k) * width % 128, 1)
                here = (group >= j * width) & (group < (j + 1) * width)
                result = jnp.where(here, turned, result)
        results.append(result)
    return results


def whole_block(array):
    return pl.BlockSpec(array.shape, lambda t: (0,) * array.ndim)


LIMIT = 56 * 1024 * 1024


def forward(divergence, fourier, lane, facts, blocks):
    _, bx, nl, ny = divergence.shape
    tile = min(256, ny)
    lx, s0, lam, e0, e1 = local_tables(bx, nl, tile)
    even, odd = parity_tables(bx, nl)
    kh, kl = split_table(np.stack([even.T, odd.T]))
    fh, fl = split_table(fourier.T)
    across = pl.BlockSpec((ny, tile), lambda t: (0, t))
    cells = bx * nl
    count = 2 * bx + 2 * nl
    rows_shape = jax.ShapeDtypeStruct((count, ny), jnp.float32)
    rows_spec = pl.BlockSpec((count, tile), lambda t: (0, t))
    scratch = [pltpu.VMEM((cells, ny), jnp.bfloat16)] * 2
    if blocks:
        rows_shape = jax.ShapeDtypeStruct((blocks, bx + 8, 128), jnp.float32)
        rows_spec = pl.BlockSpec((blocks * tile // ny, bx + 8, 128), lambda t: (t, 0, 0))
        scratch = [pltpu.VMEM((count, tile), jnp.float32)] + scratch
    return pl.pallas_call(
        functools.partial(forward_kernel, bx, nl, lx, s0),
        grid=(ny // tile,),
        out_shape=[jax.ShapeDtypeStruct((cells, ny), jnp.float32), rows_shape],
        in_specs=[whole_block(divergence), across, across]
        + [whole_block(a) for a in (kh, kl, lam, e0, e1)]
        + [pl.BlockSpec((8, tile), lambda t: (0, t)), whole_block(facts)],
        out_specs=[pl.BlockSpec((cells, tile), lambda t: (0, t)), rows_spec],
        scratch_shapes=scratch,
        compiler_params=pltpu.CompilerParams(vmem_limit_bytes=LIMIT),
        name="forward",
    )(divergence, fh, fl, kh, kl, lam, e0, e1, lane, facts)


def inverse(vhat, rows, weighted, lane, shape):
    _, bx, nl, ny = shape
    tile = min(256, ny)
    lx, s0, lam, e0, e1 = local_tables(bx, nl, tile)
    even, odd = parity_tables(bx, nl)
    kh, kl = split_table(np.stack([even, odd]))
    fh, fl = split_table(weighted)
    across = pl.BlockSpec((ny, tile), lambda t: (0, t))
    cells = bx * nl
    scratch = [pltpu.VMEM((cells, ny), jnp.bfloat16)] * 2
    if rows.ndim == 3:
        scratch = scratch + [pltpu.VMEM((2 * bx + 2 * nl, ny), jnp.float32)]
    return pl.pallas_call(
        functools.partial(inverse_kernel, bx, nl, lx, s0, tile),
        grid=(ny // tile,),
        out_shape=jax.ShapeDtypeStruct(shape, jnp.float32),
        in_specs=[whole_block(vhat), whole_block(rows), across, across]
        + [whole_block(a) for a in (kh, kl, lam, e0, e1, lane)],
        out_specs=pl.BlockSpec((1, bx, nl, tile), lambda t: (0, 0, 0, t)),
        scratch_shapes=scratch,
        compiler_params=pltpu.CompilerParams(vmem_limit_bytes=LIMIT),
        name="inverse",
    )(vhat, rows, fh, fl, kh, kl, lam, e0, e1, lane)


def face_response(mu, extent):
    half = 0.5 * mu
    rho = 1.0 / (1.0 + half + jnp.sqrt(mu + half * half))
    rho2 = rho * rho
    power = jnp.ones_like(rho)
    base, left = rho, extent
    while left:
        if left & 1:
            power = power * base
        base, left = base * base, left >> 1
    scale = 1.0 / (1.0 - power * power * rho2)
    return rho * (1.0 - power * power) * scale, power * (1.0 - rho2) * scale


def split3(array):
    high, low = split(array)
    rest = array - high.astype(jnp.float32) - low.astype(jnp.float32)
    return high, low, rest.astype(jnp.bfloat16)


def moved(values, hot):
    first, second, third = (
        jnp.dot(part, hot, preferred_element_type=jnp.float32) for part in split3(values)
    )
    return first + (second + third)


def middle_kernel(
    bx, nz, lx, s0, jump, a0, a1, rows, slots, lift_table, end_h, end_l, to_h, to_l, from_h, from_l,
    lz, zsum, west_out, east_out, inner, lift,
):
    half = bx // 2
    lanes = a0.shape[1]
    west_slot, east_slot = rows[0:1, :], rows[1:2, :]
    stiffness, twice = rows[2:3, :], rows[3:4, :] > 0.5
    shift, ratio = rows[4:5, :], rows[5:6, :]
    mu = lz[...] + ratio
    lift_rows = lift_table[...]

    sums = []
    for part in range(2):
        total = jnp.zeros((nz, lanes), jnp.float32)
        for c in range(half):
            i = part * half + c
            high, low = split(jump[i])
            both = jnp.concatenate([high, low, high])
            value = jnp.dot(lift_rows, both, preferred_element_type=jnp.float32)
            value = value * inverse_of(mu + lx[i])
            lift[i] = value
            total = total + s0[i] * value
        sums.append(total)
    first_face = dot3(to_h[...], to_l[...], *split(a0[...])) + sums[0] + sums[1]
    last_face = dot3(to_h[...], to_l[...], *split(a1[...])) + sums[0] - sums[1]

    west_hot = jnp.where(slots[...] == west_slot, 1.0, 0.0)
    east_hot = jnp.where(slots[...] == east_slot, 1.0, 0.0)
    link = (west_hot + east_hot).astype(jnp.bfloat16)
    west_hot, east_hot = west_hot.astype(jnp.bfloat16), east_hot.astype(jnp.bfloat16)
    direct, across = face_response(mu, bx)
    weight = zsum[...]

    def sweep(west, east):
        return (
            first_face + direct * west + across * east,
            last_face + across * west + direct * east,
        )

    used_w, used_e = moved(last_face, west_hot), moved(first_face, east_hot)
    second = sweep(used_w, used_e)
    first = jnp.where(twice, second[0], first_face)
    last = jnp.where(twice, second[1], last_face)
    west, east = moved(last, west_hot), moved(first, east_hot)
    change = west + east - jnp.where(twice, used_w + used_e, 0.0)
    rhs = jnp.sum(change * weight, axis=0, keepdims=True) * stiffness
    diagonal = stiffness * float(2 * nz + 2 * bx) + float(bx * nz) * shift
    coupling = stiffness * float(nz)
    spread = jnp.zeros((16, lanes), jnp.float32)
    rhs, diagonal, coupling = rhs + spread, diagonal + spread, coupling + spread
    step = DAMPING / diagonal
    correction = step * rhs
    for _ in range(CITERS - 1):
        linked = moved(correction, link)
        correction = correction + step * (rhs - diagonal * correction + coupling * linked)
    west = west + moved(correction, west_hot)[0:1] * weight
    east = east + moved(correction, east_hot)[0:1] * weight
    first, last = sweep(west, east)
    west = jnp.where(twice, moved(last, west_hot), west)
    east = jnp.where(twice, moved(first, east_hot), east)

    west_out[...] = dot3(from_h[...], from_l[...], *split(west))
    east_out[...] = dot3(from_h[...], from_l[...], *split(east))
    for part in range(2):
        face = west + east if part == 0 else west - east
        for c in range(half):
            i = part * half + c
            total = lift[i] + (s0[i] * face) * inverse_of(mu + lx[i])
            inner[i] = dot3(end_h[...], end_l[...], *split(total))


def middle(got, sweeps, k, bx, nl, modes, columns):
    nz = nl * modes
    share = k.shape[0] // (modes * columns)
    me = lax.axis_index("mode") * columns + lax.axis_index("blk")
    own_k = jnp.tile(lax.dynamic_slice_in_dim(k, me * share, share), columns)
    sx, lx = sine_table(bx)
    sz, lz = sine_table(nz)
    sl, _ = sine_table(nl)
    to_global = sz @ np.kron(np.eye(modes), sl)
    picks = [r for d in range(1, modes) for r in (d * nl - 1, d * nl)]
    order = parity_order(bx)
    ends = np.zeros((-(-len(picks) // 16) * 16, nz))
    ends[: len(picks)] = sz[picks]
    end_h, end_l = split_table(ends)
    to_h, to_l = split_table(to_global)
    from_h, from_l = split_table(to_global.T)
    lift_table = jnp.concatenate([end_h.T, end_h.T, end_l.T], axis=1)
    grouped = 4 * share == 128 and bx == nl
    if grouped:
        got = got.reshape(modes, columns, bx + 8, 4, share).transpose(0, 3, 2, 1, 4)
        got = got.reshape(modes, 4, bx + 8, columns * share)
        facts = got[0, :3, bx]
        got = got[:, :, :bx].reshape(modes, 4 * bx, columns * share)
    else:
        got = [unpack(got[d * columns : (d + 1) * columns], share) for d in range(modes)]
        got = jnp.stack(got)
        facts = got[0, 2 * bx + 2 * nl : 2 * bx + 2 * nl + 3]
    lanes = got.shape[2]
    vf, vl = got[:, :bx], got[:, bx : 2 * bx]
    a0 = got[:, 2 * bx : 2 * bx + nl].reshape(nz, lanes)
    a1 = got[:, 2 * bx + nl : 2 * bx + 2 * nl].reshape(nz, lanes)
    level = facts[2].astype(jnp.int32)
    level_ids = jnp.arange(sweeps.shape[0], dtype=jnp.int32)
    allowed = jnp.sum(jnp.where(level[:, None] == level_ids, sweeps, 0), axis=1)
    s = jnp.left_shift(jnp.ones_like(level), 2 * level).astype(jnp.float32)
    twice = (allowed > 1).astype(jnp.float32)
    rows = jnp.stack([facts[0], facts[1], s, twice, own_k, own_k / s, s, s])
    slot, within = np.arange(lanes) // share, np.arange(lanes) % share
    slots = f32(np.where(within[:, None] == within[None, :], slot[:, None], -2))
    jump = [t for d in range(1, modes) for t in (vf[d], vl[d - 1])]
    jump += [jnp.zeros_like(vf[0])] * (ends.shape[0] - len(picks))
    jump = jnp.stack(jump, axis=1)
    west, east, inner = pl.pallas_call(
        functools.partial(
            middle_kernel,
            bx,
            nz,
            tuple(float(lx[i]) for i in order),
            tuple(float(sx[0, i]) for i in order),
        ),
        out_shape=[
            jax.ShapeDtypeStruct((nz, lanes), jnp.float32),
            jax.ShapeDtypeStruct((nz, lanes), jnp.float32),
            jax.ShapeDtypeStruct((bx, ends.shape[0], lanes), jnp.float32),
        ],
        in_specs=[pl.BlockSpec(memory_space=pltpu.VMEM)] * 14,
        out_specs=[pl.BlockSpec(memory_space=pltpu.VMEM)] * 3,
        scratch_shapes=[pltpu.VMEM((bx, nz, lanes), jnp.float32)],
        compiler_params=pltpu.CompilerParams(vmem_limit_bytes=32 * 1024 * 1024),
        name="middle",
    )(
        jump, a0, a1, rows, slots, lift_table, end_h, end_l, to_h, to_l, from_h, from_l,
        f32(lz[:, None]), f32(sz.sum(axis=0)[:, None]),
    )
    west, east = west.reshape(modes, nl, lanes), east.reshape(modes, nl, lanes)
    none = jnp.zeros((bx, lanes), jnp.float32)
    parcels = []
    for d in range(modes):
        below = none if d == 0 else inner[:, 2 * d - 2] + vl[d - 1]
        above = none if d == modes - 1 else inner[:, 2 * d + 1] + vf[d + 1]
        if grouped:
            parcel = jnp.stack([below, above, west[d], east[d]]).reshape(4, bx, columns, share)
            parcels.append(parcel.transpose(2, 1, 0, 3).reshape(columns, bx, 128))
        else:
            parcels.append(pack(jnp.concatenate([below, above, west[d], east[d]]), columns))
    return jnp.concatenate(parcels)


def body(divergence, neighbours, levels, sweeps):
    _, bx, nl, ny = divergence.shape
    modes = lax.axis_size("mode")
    columns = lax.axis_size("blk")
    share = ny // (modes * columns)
    fourier, weights, shift = fourier_table(ny)
    k = f32(shift)
    inv_s = jnp.right_shift(jnp.full_like(levels, 1 << 20), 2 * levels).astype(jnp.float32)[0]
    inv_s = inv_s * (0.5**20)
    lane = jnp.concatenate([(k * inv_s)[None], jnp.full((7, ny), inv_s)])
    n = modes * columns
    facts = jnp.concatenate([neighbours[0], levels]).astype(jnp.float32)
    table = weights[:, None] * fourier
    if 4 * share == 128 and bx == nl:
        tag = jnp.concatenate([jnp.repeat(facts, share), jnp.zeros((share,), jnp.float32)])
        tag = jnp.broadcast_to(tag[None], (8, 128))
        vhat, parcels = forward(divergence, fourier, lane, tag, n)
        back = exchange(middle(exchange(parcels, 0), sweeps, k, bx, nl, modes, columns), 1)
        return inverse(vhat, back, table, lane, divergence.shape)
    vhat, out = forward(divergence, fourier, lane, jnp.zeros((8, 128), jnp.float32), 0)
    extra = -(2 * bx + 2 * nl + 3) % (128 // share) + 3
    facts = jnp.concatenate([facts, jnp.zeros((extra - 3,), jnp.float32)])
    out = jnp.concatenate([out, jnp.broadcast_to(facts[:, None], (extra, ny))])
    got = exchange(pack(out, n), 0)
    back = exchange(middle(got, sweeps, k, bx, nl, modes, columns), 1)
    return inverse(vhat, unpack(back, share), table, lane, divergence.shape)


def solution(mesh):
    return jax.shard_map(
        body,
        mesh=mesh,
        in_specs=(P("blk", None, "mode", None), P("blk", None), P("blk"), P()),
        out_specs=P("blk", None, "mode", None),
        check_vma=False,
    )
```

```python
import functools

import jax
import jax.numpy as jnp
import ml_dtypes
import numpy as np
from jax import lax
from jax.experimental import pallas as pl
from jax.experimental.pallas import tpu as pltpu
from jax.sharding import PartitionSpec as P

SWEEPS = 2
CITERS = 8
DAMPING = 0.8


def sine_table(extent):
    ordinal = np.arange(1, extent + 1)
    phases = np.outer(ordinal, ordinal) % (2 * (extent + 1))
    matrix = np.sqrt(2.0 / (extent + 1)) * np.sin(phases * (np.pi / (extent + 1)))
    eigen = 2.0 - 2.0 * np.cos(ordinal * (np.pi / (extent + 1)))
    return matrix, eigen


def fourier_table(length):
    half = length // 2
    ids = np.arange(length)
    wave = np.where(ids <= half, ids, ids - half)
    angles = (np.outer(wave, ids) % length) * (2.0 * np.pi / length)
    fourier = np.where((ids <= half)[:, None], np.cos(angles), np.sin(angles))
    weights = np.where((ids == 0) | (ids == half), 1.0, 2.0) / length
    shift = 2.0 - 2.0 * np.cos(wave * (2.0 * np.pi / length))
    return fourier, weights, shift


def f32(array):
    return jnp.asarray(np.asarray(array, np.float32))


def exchange_kernel(columns, n, src, dst, send_sem, recv_sem, own_sem):
    me = lax.axis_index("mode") * columns + lax.axis_index("blk")

    def place(slot):
        return {"mode": slot // columns, "blk": lax.rem(slot, columns)}

    def send(step):
        peer = lax.rem(me + step, n)
        return pltpu.make_async_remote_copy(
            src_ref=src.at[peer],
            dst_ref=dst.at[me],
            send_sem=send_sem.at[step],
            recv_sem=recv_sem.at[step],
            device_id=place(peer),
            device_id_type=pl.DeviceIdType.MESH,
        )

    barrier = pltpu.get_barrier_semaphore()

    @pl.loop(1, n)
    def _(step):
        pl.semaphore_signal(
            barrier,
            inc=1,
            device_id=place(lax.rem(me + step, n)),
            device_id_type=pl.DeviceIdType.MESH,
        )

    own = pltpu.make_async_copy(src.at[me], dst.at[me], own_sem)
    own.start()
    pl.semaphore_wait(barrier, n - 1)

    @pl.loop(1, n)
    def _(step):
        send(step).start()

    own.wait()

    @pl.loop(1, n)
    def _(step):
        send(step).wait()


def exchange(values, number):
    columns = lax.axis_size("blk")
    n = lax.axis_size("mode") * columns
    return pl.pallas_call(
        functools.partial(exchange_kernel, columns, n),
        out_shape=jax.ShapeDtypeStruct(values.shape, values.dtype),
        in_specs=[pl.BlockSpec(memory_space=pltpu.VMEM)],
        out_specs=pl.BlockSpec(memory_space=pltpu.VMEM),
        scratch_shapes=[
            pltpu.SemaphoreType.DMA((n,)),
            pltpu.SemaphoreType.DMA((n,)),
            pltpu.SemaphoreType.DMA,
        ],
        compiler_params=pltpu.CompilerParams(collective_id=number, has_side_effects=True),
        name=f"exchange_{number}",
    )(values)


def pack(rows, blocks):
    share = rows.shape[1] // blocks
    rows = rows.reshape(rows.shape[0], blocks, share).transpose(1, 0, 2)
    return rows.reshape(blocks, -1, 128)


def unpack(parcels, share):
    blocks = parcels.shape[0]
    rows = parcels.reshape(blocks, -1, share).transpose(1, 0, 2)
    return rows.reshape(-1, blocks * share)


def split(array):
    high = array.astype(jnp.bfloat16)
    return high, (array - high.astype(jnp.float32)).astype(jnp.bfloat16)


def split_table(array):
    array = np.asarray(array, np.float32)
    high = array.astype(ml_dtypes.bfloat16)
    low = (array - high.astype(np.float32)).astype(ml_dtypes.bfloat16)
    return jnp.asarray(high), jnp.asarray(low)


def dot3(a_high, a_low, b_high, b_low):
    def dot(a, b):
        return jnp.dot(a, b, preferred_element_type=jnp.float32)

    return dot(a_high, b_high) + (dot(a_high, b_low) + dot(a_low, b_high))


def inverse_of(value):
    guess = pl.reciprocal(value, approx=True)
    return guess * (2.0 - value * guess)


def parity_order(bx):
    return list(range(0, bx, 2)) + list(range(1, bx, 2))


def parity_tables(bx, nl):
    sx, _ = sine_table(bx)
    sl, _ = sine_table(nl)
    return [np.kron(sx[: bx // 2, part::2], sl) for part in (0, 1)]


def forward_kernel(bx, nl, lx, s0, x, fh, fl, kh, kl, lam, e0, e1, lane, facts, vhat, *rest):
    parcels, rows, ah, al = rest if len(rest) == 4 else (None,) + rest
    half = bx // 2
    side = half * nl

    @pl.when(pl.program_id(0) == 0)
    def _():
        for c in range(half):
            top, bottom = x[0, c], x[0, bx - 1 - c]
            for part, value in ((0, top + bottom), (1, top - bottom)):
                high, low = split(value)
                ah[pl.ds((part * half + c) * nl, nl), :] = high
                al[pl.ds((part * half + c) * nl, nl), :] = low

    base = lam[...] + lane[0:1, :]
    scale = lane[1:2, :]
    sums = []
    for part in range(2):
        own = pl.ds(part * side, side)
        spectrum = dot3(ah[own, :], al[own, :], fh[...], fl[...])
        high, low = split(spectrum)
        ghat = dot3(kh[part], kl[part], high, low)
        total = None
        for c in range(half):
            i = part * half + c
            value = ghat[c * nl : (c + 1) * nl] * (scale * inverse_of(base + lx[i]))
            vhat[pl.ds(i * nl, nl), :] = value
            rows[pl.ds(i, 1), :] = jnp.sum(value * e0[...], axis=0, keepdims=True)
            rows[pl.ds(bx + i, 1), :] = jnp.sum(value * e1[...], axis=0, keepdims=True)
            term = value * s0[i]
            total = term if total is None else total + term
        sums.append(total)
    rows[pl.ds(2 * bx, nl), :] = sums[0] + sums[1]
    rows[pl.ds(2 * bx + nl, nl), :] = sums[0] - sums[1]
    if parcels is not None:
        for h in range(parcels.shape[0] // 4):
            here = pl.ds(h * 128, 128)
            groups = lane_groups([rows[pl.ds(g * bx, bx), here] for g in range(4)])
            for c in range(4):
                parcels[h * 4 + c, pl.ds(0, bx), :] = groups[c]
                parcels[h * 4 + c, pl.ds(bx, 8), :] = facts[...]


def inverse_kernel(bx, nl, lx, s0, tile, vhat, got, fh, fl, kh, kl, lam, e0, e1, lane, out, uh, ul, *rest):
    rows = rest[0] if rest else got
    half = bx // 2
    side = half * nl

    @pl.when(pl.program_id(0) == 0)
    def _():
        if rest:
            for h in range(got.shape[0] // 4):
                groups = lane_groups([got[h * 4 + c] for c in range(4)])
                for g in range(4):
                    rows[pl.ds(g * bx, bx), pl.ds(h * 128, 128)] = groups[g]

        @pl.loop(0, vhat.shape[1] // tile)
        def _(step):
            q = pl.ds(pl.multiple_of(step * tile, tile), tile)
            base = lam[...] + lane[0:1, q]
            west, east = rows[pl.ds(2 * bx, nl), q], rows[pl.ds(2 * bx + nl, nl), q]
            for part in range(2):
                face = west + east if part == 0 else west - east
                parts = []
                for c in range(half):
                    i = part * half + c
                    load = (
                        face * s0[i] + rows[pl.ds(i, 1), q] * e0[...] + rows[pl.ds(bx + i, 1), q] * e1[...]
                    )
                    parts.append(vhat[pl.ds(i * nl, nl), q] + load * inverse_of(base + lx[i]))
                high, low = split(jnp.concatenate(parts))
                high, low = split(dot3(kh[part], kl[part], high, low))
                uh[pl.ds(part * side, side), q] = high
                ul[pl.ds(part * side, side), q] = low

    even = dot3(uh[pl.ds(0, side), :], ul[pl.ds(0, side), :], fh[...], fl[...])
    odd = dot3(uh[pl.ds(side, side), :], ul[pl.ds(side, side), :], fh[...], fl[...])
    for c in range(half):
        here = slice(c * nl, (c + 1) * nl)
        out[0, c] = even[here] + odd[here]
        out[0, bx - 1 - c] = even[here] - odd[here]


def local_tables(bx, nl, tile):
    sx, lx = sine_table(bx)
    sl, ll = sine_table(nl)
    order = parity_order(bx)
    return (
        tuple(float(lx[i]) for i in order),
        tuple(float(sx[0, i]) for i in order),
        f32(np.tile(ll[:, None], (1, tile))),
        f32(np.tile(sl[0][:, None], (1, tile))),
        f32(np.tile(sl[-1][:, None], (1, tile))),
    )


def lane_groups(arrays):
    count = len(arrays)
    width = 128 // count
    group = lax.broadcasted_iota(jnp.int32, arrays[0].shape, 1)
    results = []
    for k in range(count):
        result = arrays[k]
        for j in range(count):
            if j != k:
                turned = pltpu.roll(arrays[j], (j - k) * width % 128, 1)
                here = (group >= j * width) & (group < (j + 1) * width)
                result = jnp.where(here, turned, result)
        results.append(result)
    return results


def whole_block(array):
    return pl.BlockSpec(array.shape, lambda t: (0,) * array.ndim)


LIMIT = 56 * 1024 * 1024


def forward(divergence, fourier, lane, facts, blocks):
    _, bx, nl, ny = divergence.shape
    tile = min(256, ny)
    lx, s0, lam, e0, e1 = local_tables(bx, nl, tile)
    even, odd = parity_tables(bx, nl)
    kh, kl = split_table(np.stack([even.T, odd.T]))
    fh, fl = split_table(fourier.T)
    across = pl.BlockSpec((ny, tile), lambda t: (0, t))
    cells = bx * nl
    count = 2 * bx + 2 * nl
    rows_shape = jax.ShapeDtypeStruct((count, ny), jnp.float32)
    rows_spec = pl.BlockSpec((count, tile), lambda t: (0, t))
    scratch = [pltpu.VMEM((cells, ny), jnp.bfloat16)] * 2
    if blocks:
        rows_shape = jax.ShapeDtypeStruct((blocks, bx + 8, 128), jnp.float32)
        rows_spec = pl.BlockSpec((blocks * tile // ny, bx + 8, 128), lambda t: (t, 0, 0))
        scratch = [pltpu.VMEM((count, tile), jnp.float32)] + scratch
    return pl.pallas_call(
        functools.partial(forward_kernel, bx, nl, lx, s0),
        grid=(ny // tile,),
        out_shape=[jax.ShapeDtypeStruct((cells, ny), jnp.float32), rows_shape],
        in_specs=[whole_block(divergence), across, across]
        + [whole_block(a) for a in (kh, kl, lam, e0, e1)]
        + [pl.BlockSpec((8, tile), lambda t: (0, t)), whole_block(facts)],
        out_specs=[pl.BlockSpec((cells, tile), lambda t: (0, t)), rows_spec],
        scratch_shapes=scratch,
        compiler_params=pltpu.CompilerParams(vmem_limit_bytes=LIMIT),
        name="forward",
    )(divergence, fh, fl, kh, kl, lam, e0, e1, lane, facts)


def inverse(vhat, rows, weighted, lane, shape):
    _, bx, nl, ny = shape
    tile = min(256, ny)
    lx, s0, lam, e0, e1 = local_tables(bx, nl, tile)
    even, odd = parity_tables(bx, nl)
    kh, kl = split_table(np.stack([even, odd]))
    fh, fl = split_table(weighted)
    across = pl.BlockSpec((ny, tile), lambda t: (0, t))
    cells = bx * nl
    scratch = [pltpu.VMEM((cells, ny), jnp.bfloat16)] * 2
    if rows.ndim == 3:
        scratch = scratch + [pltpu.VMEM((2 * bx + 2 * nl, ny), jnp.float32)]
    return pl.pallas_call(
        functools.partial(inverse_kernel, bx, nl, lx, s0, tile),
        grid=(ny // tile,),
        out_shape=jax.ShapeDtypeStruct(shape, jnp.float32),
        in_specs=[whole_block(vhat), whole_block(rows), across, across]
        + [whole_block(a) for a in (kh, kl, lam, e0, e1, lane)],
        out_specs=pl.BlockSpec((1, bx, nl, tile), lambda t: (0, 0, 0, t)),
        scratch_shapes=scratch,
        compiler_params=pltpu.CompilerParams(vmem_limit_bytes=LIMIT),
        name="inverse",
    )(vhat, rows, fh, fl, kh, kl, lam, e0, e1, lane)


def face_response(mu, extent):
    half = 0.5 * mu
    rho = 1.0 / (1.0 + half + jnp.sqrt(mu + half * half))
    rho2 = rho * rho
    power = jnp.ones_like(rho)
    base, left = rho, extent
    while left:
        if left & 1:
            power = power * base
        base, left = base * base, left >> 1
    scale = 1.0 / (1.0 - power * power * rho2)
    return rho * (1.0 - power * power) * scale, power * (1.0 - rho2) * scale


def split3(array):
    high, low = split(array)
    rest = array - high.astype(jnp.float32) - low.astype(jnp.float32)
    return high, low, rest.astype(jnp.bfloat16)


def moved(values, hot):
    first, second, third = (
        jnp.dot(part, hot, preferred_element_type=jnp.float32) for part in split3(values)
    )
    return first + (second + third)


def middle_kernel(
    bx, nz, lx, s0, jump, a0, a1, rows, slots, lift_table, end_h, end_l, to_h, to_l, from_h, from_l,
    lz, zsum, west_out, east_out, inner, lift,
):
    half = bx // 2
    lanes = a0.shape[1]
    west_slot, east_slot = rows[0:1, :], rows[1:2, :]
    stiffness, twice = rows[2:3, :], rows[3:4, :] > 0.5
    shift, ratio = rows[4:5, :], rows[5:6, :]
    mu = lz[...] + ratio
    lift_rows = lift_table[...]

    sums = []
    for part in range(2):
        total = jnp.zeros((nz, lanes), jnp.float32)
        for c in range(half):
            i = part * half + c
            high, low = split(jump[i])
            both = jnp.concatenate([high, low, high])
            value = jnp.dot(lift_rows, both, preferred_element_type=jnp.float32)
            value = value * inverse_of(mu + lx[i])
            lift[i] = value
            total = total + s0[i] * value
        sums.append(total)
    first_face = dot3(to_h[...], to_l[...], *split(a0[...])) + sums[0] + sums[1]
    last_face = dot3(to_h[...], to_l[...], *split(a1[...])) + sums[0] - sums[1]

    west_hot = jnp.where(slots[...] == west_slot, 1.0, 0.0)
    east_hot = jnp.where(slots[...] == east_slot, 1.0, 0.0)
    link = (west_hot + east_hot).astype(jnp.bfloat16)
    west_hot, east_hot = west_hot.astype(jnp.bfloat16), east_hot.astype(jnp.bfloat16)
    direct, across = face_response(mu, bx)
    weight = zsum[...]

    def sweep(west, east):
        return (
            first_face + direct * west + across * east,
            last_face + across * west + direct * east,
        )

    used_w, used_e = moved(last_face, west_hot), moved(first_face, east_hot)
    second = sweep(used_w, used_e)
    first = jnp.where(twice, second[0], first_face)
    last = jnp.where(twice, second[1], last_face)
    west, east = moved(last, west_hot), moved(first, east_hot)
    change = west + east - jnp.where(twice, used_w + used_e, 0.0)
    rhs = jnp.sum(change * weight, axis=0, keepdims=True) * stiffness
    diagonal = stiffness * float(2 * nz + 2 * bx) + float(bx * nz) * shift
    coupling = stiffness * float(nz)
    spread = jnp.zeros((16, lanes), jnp.float32)
    rhs, diagonal, coupling = rhs + spread, diagonal + spread, coupling + spread
    step = DAMPING / diagonal
    correction = step * rhs
    for _ in range(CITERS - 1):
        linked = moved(correction, link)
        correction = correction + step * (rhs - diagonal * correction + coupling * linked)
    west = west + moved(correction, west_hot)[0:1] * weight
    east = east + moved(correction, east_hot)[0:1] * weight
    first, last = sweep(west, east)
    west = jnp.where(twice, moved(last, west_hot), west)
    east = jnp.where(twice, moved(first, east_hot), east)

    west_out[...] = dot3(from_h[...], from_l[...], *split(west))
    east_out[...] = dot3(from_h[...], from_l[...], *split(east))
    for part in range(2):
        face = west + east if part == 0 else west - east
        for c in range(half):
            i = part * half + c
            total = lift[i] + (s0[i] * face) * inverse_of(mu + lx[i])
            inner[i] = dot3(end_h[...], end_l[...], *split(total))


def grouped_kernel(
    bx, nl, modes, columns, levels, lx, s0, sweeps, got, own_k, slots, lift_table, end_h, end_l, to_h, to_l,
    from_h, from_l, lz, zsum, parcels, lift, parts, rows, jump, inner, a0, a1, west, east,
):
    nz = nl * modes
    for d in range(modes):
        for h in range(columns // 4):
            here = pl.ds(h * 128, 128)
            groups = lane_groups([got[d * columns + h * 4 + c] for c in range(4)])
            for g in range(2):
                parts[d, g, :, here] = groups[g][:bx]
            a0[pl.ds(d * nl, nl), here] = groups[2][:nl]
            a1[pl.ds(d * nl, nl), here] = groups[3][:nl]
            if d == 0:
                for g in range(3):
                    rows[pl.ds(g, 1), here] = groups[g][bx : bx + 1]
    level = rows[2:3, :]
    stiffness = jnp.zeros_like(level)
    allowed = jnp.zeros_like(level)
    for number in range(levels):
        stiffness = jnp.where(level == float(number), float(4**number), stiffness)
        allowed = jnp.where(level == float(number), sweeps[number].astype(jnp.float32), allowed)
    rows[2:3, :] = stiffness
    rows[3:4, :] = jnp.where(allowed > 1.5, 1.0, 0.0)
    rows[4:5, :] = own_k[0:1, :]
    rows[5:6, :] = own_k[0:1, :] / stiffness
    jump[...] = jnp.zeros(jump.shape, jnp.float32)
    for d in range(1, modes):
        for i in range(bx):
            jump[i, pl.ds(2 * d - 2, 1), :] = parts[d, 0, pl.ds(i, 1), :]
            jump[i, pl.ds(2 * d - 1, 1), :] = parts[d - 1, 1, pl.ds(i, 1), :]
    middle_kernel(
        bx, nz, lx, s0, jump, a0, a1, rows, slots, lift_table, end_h, end_l, to_h, to_l, from_h, from_l,
        lz, zsum, west, east, inner, lift,
    )
    for d in range(1, modes):
        for i in range(bx):
            one = pl.ds(i, 1)
            parts[d - 1, 1, one, :] = parts[d - 1, 1, one, :] + inner[i, pl.ds(2 * d - 2, 1), :]
            parts[d, 0, one, :] = parts[d, 0, one, :] + inner[i, pl.ds(2 * d - 1, 1), :]
    none = jnp.zeros((bx, 128), jnp.float32)
    for d in range(modes):
        for h in range(columns // 4):
            here = pl.ds(h * 128, 128)
            below = parts[d - 1, 1, :, here] if d > 0 else none
            above = parts[d + 1, 0, :, here] if d < modes - 1 else none
            slab = pl.ds(d * nl, nl)
            groups = lane_groups([below, above, west[slab, here], east[slab, here]])
            for c in range(4):
                parcels[d * columns + h * 4 + c] = groups[c]


def middle(got, sweeps, k, bx, nl, modes, columns):
    nz = nl * modes
    share = k.shape[0] // (modes * columns)
    me = lax.axis_index("mode") * columns + lax.axis_index("blk")
    own_k = jnp.tile(lax.dynamic_slice_in_dim(k, me * share, share), columns)
    sx, lx = sine_table(bx)
    sz, lz = sine_table(nz)
    sl, _ = sine_table(nl)
    to_global = sz @ np.kron(np.eye(modes), sl)
    picks = [r for d in range(1, modes) for r in (d * nl - 1, d * nl)]
    order = parity_order(bx)
    ends = np.zeros((-(-len(picks) // 16) * 16, nz))
    ends[: len(picks)] = sz[picks]
    end_h, end_l = split_table(ends)
    to_h, to_l = split_table(to_global)
    from_h, from_l = split_table(to_global.T)
    lift_table = jnp.concatenate([end_h.T, end_h.T, end_l.T], axis=1)
    slot, within = np.arange(columns * share) // share, np.arange(columns * share) % share
    slots = f32(np.where(within[:, None] == within[None, :], slot[:, None], -2))
    numbers = (tuple(float(lx[i]) for i in order), tuple(float(sx[0, i]) for i in order))
    tables = (
        slots, lift_table, end_h, end_l, to_h, to_l, from_h, from_l,
        f32(lz[:, None]), f32(sz.sum(axis=0)[:, None]),
    )
    grouped = 4 * share == 128 and bx == nl and columns % 4 == 0
    if grouped:
        lanes = columns * share
        own_k = jnp.broadcast_to(own_k[None], (8, lanes))
        shapes = [
            (bx, nz, lanes), (modes, 2, bx, lanes), (8, lanes), (bx, ends.shape[0], lanes),
            (bx, ends.shape[0], lanes), (nz, lanes), (nz, lanes), (nz, lanes), (nz, lanes),
        ]
        return pl.pallas_call(
            functools.partial(
                grouped_kernel, bx, nl, modes, columns, sweeps.shape[0], numbers[0], numbers[1]
            ),
            out_shape=jax.ShapeDtypeStruct((modes * columns, bx, 128), jnp.float32),
            in_specs=[pl.BlockSpec(memory_space=pltpu.SMEM)]
            + [pl.BlockSpec(memory_space=pltpu.VMEM)] * (2 + len(tables)),
            out_specs=pl.BlockSpec(memory_space=pltpu.VMEM),
            scratch_shapes=[pltpu.VMEM(shape, jnp.float32) for shape in shapes],
            compiler_params=pltpu.CompilerParams(vmem_limit_bytes=32 * 1024 * 1024),
            name="middle",
        )(sweeps, got, own_k, *tables)
    got = [unpack(got[d * columns : (d + 1) * columns], share) for d in range(modes)]
    got = jnp.stack(got)
    facts = got[0, 2 * bx + 2 * nl : 2 * bx + 2 * nl + 3]
    lanes = got.shape[2]
    vf, vl = got[:, :bx], got[:, bx : 2 * bx]
    a0 = got[:, 2 * bx : 2 * bx + nl].reshape(nz, lanes)
    a1 = got[:, 2 * bx + nl : 2 * bx + 2 * nl].reshape(nz, lanes)
    level = facts[2].astype(jnp.int32)
    level_ids = jnp.arange(sweeps.shape[0], dtype=jnp.int32)
    allowed = jnp.sum(jnp.where(level[:, None] == level_ids, sweeps, 0), axis=1)
    s = jnp.left_shift(jnp.ones_like(level), 2 * level).astype(jnp.float32)
    twice = (allowed > 1).astype(jnp.float32)
    rows = jnp.stack([facts[0], facts[1], s, twice, own_k, own_k / s, s, s])
    slot, within = np.arange(lanes) // share, np.arange(lanes) % share
    slots = f32(np.where(within[:, None] == within[None, :], slot[:, None], -2))
    jump = [t for d in range(1, modes) for t in (vf[d], vl[d - 1])]
    jump += [jnp.zeros_like(vf[0])] * (ends.shape[0] - len(picks))
    jump = jnp.stack(jump, axis=1)
    west, east, inner = pl.pallas_call(
        functools.partial(
            middle_kernel,
            bx,
            nz,
            tuple(float(lx[i]) for i in order),
            tuple(float(sx[0, i]) for i in order),
        ),
        out_shape=[
            jax.ShapeDtypeStruct((nz, lanes), jnp.float32),
            jax.ShapeDtypeStruct((nz, lanes), jnp.float32),
            jax.ShapeDtypeStruct((bx, ends.shape[0], lanes), jnp.float32),
        ],
        in_specs=[pl.BlockSpec(memory_space=pltpu.VMEM)] * 14,
        out_specs=[pl.BlockSpec(memory_space=pltpu.VMEM)] * 3,
        scratch_shapes=[pltpu.VMEM((bx, nz, lanes), jnp.float32)],
        compiler_params=pltpu.CompilerParams(vmem_limit_bytes=32 * 1024 * 1024),
        name="middle",
    )(
        jump, a0, a1, rows, slots, lift_table, end_h, end_l, to_h, to_l, from_h, from_l,
        f32(lz[:, None]), f32(sz.sum(axis=0)[:, None]),
    )
    west, east = west.reshape(modes, nl, lanes), east.reshape(modes, nl, lanes)
    none = jnp.zeros((bx, lanes), jnp.float32)
    parcels = []
    for d in range(modes):
        below = none if d == 0 else inner[:, 2 * d - 2] + vl[d - 1]
        above = none if d == modes - 1 else inner[:, 2 * d + 1] + vf[d + 1]
        parcels.append(pack(jnp.concatenate([below, above, west[d], east[d]]), columns))
    return jnp.concatenate(parcels)


def body(divergence, neighbours, levels, sweeps):
    _, bx, nl, ny = divergence.shape
    modes = lax.axis_size("mode")
    columns = lax.axis_size("blk")
    share = ny // (modes * columns)
    fourier, weights, shift = fourier_table(ny)
    k = f32(shift)
    inv_s = jnp.right_shift(jnp.full_like(levels, 1 << 20), 2 * levels).astype(jnp.float32)[0]
    inv_s = inv_s * (0.5**20)
    lane = jnp.concatenate([(k * inv_s)[None], jnp.full((7, ny), inv_s)])
    n = modes * columns
    facts = jnp.concatenate([neighbours[0], levels]).astype(jnp.float32)
    table = weights[:, None] * fourier
    if 4 * share == 128 and bx == nl and columns % 4 == 0:
        tag = jnp.concatenate([jnp.repeat(facts, share), jnp.zeros((share,), jnp.float32)])
        tag = jnp.broadcast_to(tag[None], (8, 128))
        vhat, parcels = forward(divergence, fourier, lane, tag, n)
        back = exchange(middle(exchange(parcels, 0), sweeps, k, bx, nl, modes, columns), 1)
        return inverse(vhat, back, table, lane, divergence.shape)
    vhat, out = forward(divergence, fourier, lane, jnp.zeros((8, 128), jnp.float32), 0)
    extra = -(2 * bx + 2 * nl + 3) % (128 // share) + 3
    facts = jnp.concatenate([facts, jnp.zeros((extra - 3,), jnp.float32)])
    out = jnp.concatenate([out, jnp.broadcast_to(facts[:, None], (extra, ny))])
    got = exchange(pack(out, n), 0)
    back = exchange(middle(got, sweeps, k, bx, nl, modes, columns), 1)
    return inverse(vhat, unpack(back, share), table, lane, divergence.shape)


def solution(mesh):
    return jax.shard_map(
        body,
        mesh=mesh,
        in_specs=(P("blk", None, "mode", None), P("blk", None), P("blk"), P()),
        out_specs=P("blk", None, "mode", None),
        check_vma=False,
    )
```
